256 devices in a mesh: freq: 16 (over y, x), beam: 16 (over z, core).
Axes of the slice: x: 4, y: 4, z: 8, core: 2. Of those that a mesh axis runs over, the one named last changes fastest.
Arguments:
- voltages: bfloat16 [2, 256, 16, 16384], P(None, 'beam', None, 'freq'), may hold values from -6 to 6
- gains: float32 [2, 256, 16384], P(None, 'beam', 'freq'), may hold values from -6 to 6
- shifts: int32 [12, 4096], P(None, 'freq'), may hold values from 0 to 8, as said below
- widths: int32 [8], replicated, may hold values from 1 to 16, as said below
Outputs:
- dedispersed: bfloat16 [256, 16, 4096], P('beam', None, 'freq')
- peaks: float32 [8, 256, 4096], P(None, 'beam', 'freq')
The draws below stay inside these ranges and needn't reach their ends.
Inputs may be any that keep to these rules, and one draw needn't show every extreme that they name: shifts[s, r] lies between 0 and min(2^s, 8); the last section reaches 8. widths[0] is 1, widths[k] lies between 2^(k-1) + 1 and 2^k capped at 16, and the last is 16.
All inputs are finite; a program needn't handle non-finite values.
Results may differ from the reference program's by a relative error of at most 0.0091.
Values may be sent and summed in bfloat16 or wider, within the bound.
No kernel may reach another device: no remote copies, remote signals or barrier semaphores. Data moves between devices by JAX's collectives and lax.ppermute only.
A program may use at most 128 MiB of HBM per device.

```python
import math
import jax
import jax.numpy as jnp
from jax import lax

FEEDS = 256
SECTIONS = 12
CHAN_SUM = 4
NBOX = 8
TIME = 16
BEAMS = 256
NSUB = 4096
CHANNELS = 16384
SMAX = 8
WMAX = 16


def draw_shifts(key, part):
    section_rows = []
    for section_index in range(SECTIONS):
        ceiling = min(2 ** section_index, SMAX)
        section_rows.append(jax.random.randint(jax.random.fold_in(key, section_index), (NSUB,), 0, ceiling + 1, dtype=jnp.int32))
    shift_table = jnp.stack(section_rows)
    return shift_table.at[SECTIONS - 1, 0].set(SMAX)


def draw_widths(key, part):
    pieces = [jnp.ones((1,), jnp.int32)]
    for width_index in range(1, NBOX - 1):
        lowest = 2 ** (width_index - 1) + 1
        drawn = jax.random.randint(jax.random.fold_in(key, width_index), (1,), lowest, 2 ** width_index + 1, dtype=jnp.int32)
        pieces.append(jnp.minimum(drawn, WMAX))
    pieces.append(jnp.full((1,), WMAX, jnp.int32))
    return jnp.concatenate(pieces)


def block_levels(key, shape, split, low, high):
    def one(position, parts):
        steps = jax.random.uniform(jax.random.fold_in(jax.random.fold_in(key, 6), position), (parts,), jnp.float32, low / len(split), high / len(split))
        return jnp.repeat(jnp.exp(steps), shape[position] // parts).reshape((-1,) + (1,) * (len(shape) - position - 1))

    level = one(*split[0])
    for cut in split[1:]:
        level = level * one(*cut)
    return level


def noise(rng, shape, spread, most, cuts=(), held_as=jnp.bfloat16):
    result = spread * jax.random.normal(rng, shape, jnp.float32)
    if cuts:
        result = result * block_levels(rng, shape, cuts, -0.22, 0.18)
    return jnp.clip(result, -most, most).astype(held_as)


def setup_inputs(seed: int = 0) -> dict:
    keys = jax.random.split(jax.random.key(seed), 5)
    return {
        "voltages": noise(keys[0], (2, FEEDS, TIME, CHANNELS), 1.0, 6.0, ((1, 16), (3, 16))),
        "gains": noise(keys[1], (2, FEEDS, CHANNELS), 1.0, 6.0, ((1, 16), (2, 16)), jnp.float32),
        "shifts": draw_shifts(jax.random.fold_in(keys[4], 71), 0),
        "widths": draw_widths(jax.random.fold_in(keys[4], 71), 0),
    }


def steering(feed_count):
    positions = jnp.arange(feed_count, dtype=jnp.int32)
    phases = positions[:, None] * positions[None, :] % feed_count
    angles = phases.astype(jnp.float32) * (2.0 * math.pi / feed_count)
    factor = 1.0 / math.sqrt(feed_count)
    cosine = jnp.cos(angles) * factor
    sine = jnp.sin(angles) * factor
    upper_half = jnp.concatenate([cosine, sine], axis=1)
    lower_half = jnp.concatenate([-sine, cosine], axis=1)
    return jnp.concatenate([upper_half, lower_half], axis=0).astype(jnp.bfloat16)

def calibrate(voltages, gains):
    voltage_f = voltages.astype(jnp.float32)
    factor = gains[:, :, None, :]
    real_part = factor[0] * voltage_f[0] - factor[1] * voltage_f[1]
    imag_part = factor[0] * voltage_f[1] + factor[1] * voltage_f[0]
    return jnp.stack([real_part, imag_part]).astype(jnp.bfloat16)

def detect(received, matrix):
    feed_count = received.shape[1]
    samples = received.shape[2]
    local_width = received.shape[3]
    flattened = received.reshape(2 * feed_count, samples * local_width)
    formed = jnp.dot(matrix.astype(jnp.float32), flattened.astype(jnp.float32), precision=lax.Precision.HIGHEST)
    formed = formed.reshape(2, feed_count, samples, local_width)
    detected = formed[0] * formed[0] + formed[1] * formed[1]
    grouped = detected.reshape(feed_count, samples, local_width // CHAN_SUM, CHAN_SUM)
    return lax.optimization_barrier(jnp.sum(grouped, axis=3)).astype(jnp.bfloat16)

def shifted(values, offsets):
    length = values.shape[-2]
    sample_index = jnp.arange(length, dtype=jnp.int32)[:, None] + offsets.astype(jnp.int32)[None, :]
    clipped = jnp.broadcast_to(jnp.minimum(sample_index, length - 1), values.shape)
    picked = jnp.take_along_axis(values, clipped, axis=values.ndim - 2)
    return jnp.where(sample_index < length, picked, jnp.zeros((), values.dtype))

def merge_pair(values, offsets, half_size):
    leading = values.shape[:-1]
    row_count = values.shape[-1]
    grouped = values.reshape(leading + (row_count // (2 * half_size), 2, half_size))
    lower_rows = jnp.broadcast_to(grouped[..., 0:1, :], grouped.shape).reshape(values.shape)
    higher_rows = jnp.broadcast_to(grouped[..., 1:2, :], grouped.shape).reshape(values.shape)
    return lower_rows + shifted(higher_rows, offsets)

def boxcar_table(widths, length):
    sample_pos = jnp.arange(length, dtype=jnp.int32)
    starts = sample_pos[None, None, :]
    reach = widths.astype(jnp.int32)[None, :, None]
    covered = (sample_pos[:, None, None] >= starts) & (sample_pos[:, None, None] < starts + reach)
    kernel = covered.astype(jnp.float32).reshape(length, widths.shape[0] * length)
    inside_block = sample_pos[None, :] + widths.astype(jnp.int32)[:, None] <= length
    return (kernel, inside_block)

def reference(voltages, gains, shifts, widths):
    matrix = steering(FEEDS)
    block_count = CHANNELS // 256

    def form_block(block_index):
        start = block_index * 256
        volt_piece = lax.dynamic_slice_in_dim(voltages, start, 256, 3)
        gain_piece = lax.dynamic_slice_in_dim(gains, start, 256, 2)
        return detect(calibrate(volt_piece, gain_piece), matrix)
    stacked = lax.map(form_block, jnp.arange(block_count, dtype=jnp.int32))
    detected = jnp.transpose(stacked, (1, 2, 0, 3)).reshape(BEAMS, TIME, NSUB)
    kernel, inside_block = boxcar_table(widths, TIME)
    root_width = jnp.sqrt(widths.astype(jnp.float32))

    def one_beam(beam_power):
        values = beam_power.astype(jnp.float32)
        values = values - lax.optimization_barrier(jnp.mean(values, axis=0, keepdims=True))
        for section_index in range(SECTIONS):
            values = merge_pair(values, shifts[section_index], 2 ** section_index)
        scaled = values * (1.0 / (8.0 * math.sqrt(NSUB)))
        box_sums = jnp.dot(kernel.T, scaled, precision=lax.Precision.HIGHEST).reshape(NBOX, TIME, NSUB)
        best = lax.optimization_barrier(jnp.max(jnp.where(inside_block[:, :, None], box_sums, -1e+30), axis=1)) / root_width[:, None]
        return (scaled.astype(jnp.bfloat16), best)
    dedispersed, best = lax.map(one_beam, detected)
    return (dedispersed, jnp.transpose(best, (1, 0, 2)))
```

```python
import functools
import math

import jax
import jax.numpy as jnp
from jax import lax
from jax.experimental import pallas as pl
from jax.experimental.pallas import tpu as pltpu
from jax.sharding import PartitionSpec as P

FEEDS = 256
CHAN_SUM = 4
NSUB = 4096
TIME = 16
LANES = 128
MIB = 1024 * 1024


def steering(groups):
    size = FEEDS // groups
    row = lax.broadcasted_iota(jnp.int32, (2 * FEEDS, 2 * FEEDS), 0)
    col = lax.broadcasted_iota(jnp.int32, (2 * FEEDS, 2 * FEEDS), 1)
    beam, out_part = row % FEEDS, row // FEEDS
    feed = col // (2 * size) * size + col % size
    in_part = col // size % 2
    angles = (beam * feed % FEEDS).astype(jnp.float32) * (2.0 * math.pi / FEEDS)
    factor = 1.0 / math.sqrt(FEEDS)
    cosine = jnp.cos(angles) * factor
    sine = jnp.sin(angles) * factor
    value = jnp.where(in_part == out_part, cosine, jnp.where(out_part == 0, sine, -sine))
    return value.astype(jnp.bfloat16)


def calibrate_kernel(volt_ref, gain_ref, out_ref, scratch):
    feeds, samples, width = volt_ref.shape[1:]
    for j in range(width // LANES):
        lanes = slice(j * LANES, (j + 1) * LANES)
        for part in range(2):
            block = volt_ref[part, :, :, lanes].astype(jnp.float32)
            scratch[part, j] = block.reshape(feeds * samples, LANES)
        gain_re = gain_ref[0, :, lanes]
        gain_im = gain_ref[1, :, lanes]
        for t in range(samples):
            volt_re = scratch[0, j, pl.ds(t, feeds, stride=samples), :]
            volt_im = scratch[1, j, pl.ds(t, feeds, stride=samples), :]
            real = gain_re * volt_re - gain_im * volt_im
            imag = gain_re * volt_im + gain_im * volt_re
            out_ref[t, :feeds, lanes] = real.astype(jnp.bfloat16)
            out_ref[t, feeds:, lanes] = imag.astype(jnp.bfloat16)


def calibrate(voltages, gains):
    _, feeds, samples, width = voltages.shape
    step = 256
    return pl.pallas_call(
        calibrate_kernel,
        grid=(width // step,),
        in_specs=[
            pl.BlockSpec((2, feeds, samples, step), lambda i: (0, 0, 0, i)),
            pl.BlockSpec((2, feeds, step), lambda i: (0, 0, i)),
        ],
        out_specs=pl.BlockSpec((samples, 2 * feeds, step), lambda i: (0, 0, i)),
        out_shape=jax.ShapeDtypeStruct((samples, 2 * feeds, width), jnp.bfloat16),
        scratch_shapes=[pltpu.VMEM((2, step // LANES, feeds * samples, LANES), jnp.float32)],
        compiler_params=pltpu.CompilerParams(vmem_limit_bytes=8 * MIB),
        name="calibrate",
    )(voltages, gains)


def detect_kernel(matrix_ref, x_ref, out_ref):
    width = x_ref.shape[1]
    step = 256
    total = jnp.zeros((FEEDS, width // CHAN_SUM), jnp.float32)
    channel = lax.broadcasted_iota(jnp.int32, (step, width // CHAN_SUM), 0)
    group = lax.broadcasted_iota(jnp.int32, (step, width // CHAN_SUM), 1)
    for j in range(width // step):
        cols = slice(j * step, (j + 1) * step)
        formed = jnp.dot(matrix_ref[...], x_ref[:, cols], preferred_element_type=jnp.float32)
        power = formed[:FEEDS] * formed[:FEEDS] + formed[FEEDS:] * formed[FEEDS:]
        high = power.astype(jnp.bfloat16)
        low = (power - high.astype(jnp.float32)).astype(jnp.bfloat16)
        pooling = ((channel + j * step) // CHAN_SUM == group).astype(jnp.bfloat16)
        total += jnp.dot(high, pooling, preferred_element_type=jnp.float32)
        total += jnp.dot(low, pooling, preferred_element_type=jnp.float32)
    out_ref[...] = total.astype(jnp.bfloat16)


def detect(received, matrix):
    rows, width = received.shape
    return pl.pallas_call(
        detect_kernel,
        out_shape=jax.ShapeDtypeStruct((FEEDS, width // CHAN_SUM), jnp.bfloat16),
        compiler_params=pltpu.CompilerParams(vmem_limit_bytes=16 * MIB),
        name="detect",
    )(matrix, received)


def shifted(rows, bits):
    zero = jnp.zeros_like(rows[0])
    count = len(rows)
    for position, chosen in enumerate(bits):
        step = 1 << position
        rows = [jnp.where(chosen, rows[t + step] if t + step < count else zero, rows[t]) for t in range(count)]
    return rows


def digits(offsets, most, shape):
    wide = jnp.broadcast_to(offsets, shape)
    return [(wide >> position & 1) == 1 for position in range(most.bit_length())]


def tree_kernel(detected_ref, shifts_ref, own_ref, send_ref):
    samples, beams, width = detected_ref.shape
    lane = lax.broadcasted_iota(jnp.int32, (8, LANES), 1)
    blocks = width // LANES
    for b in range(0, beams, 8):
        values = []
        for j in range(blocks):
            lanes = slice(j * LANES, (j + 1) * LANES)
            rows = [detected_ref[t, :, lanes].astype(jnp.float32)[b : b + 8] for t in range(samples)]
            mean = functools.reduce(jnp.add, rows) * (1.0 / samples)
            values.append([row - mean for row in rows])
        for s in range(width.bit_length() - 1):
            half = 1 << s
            after = []
            for j in range(blocks):
                lanes = slice(j * LANES, (j + 1) * LANES)
                bits = digits(shifts_ref[s : s + 1, lanes], min(half, 8), (8, LANES))
                if half < LANES:
                    upper = (lane & half) != 0
                    lower_rows = [jnp.where(upper, pltpu.roll(x, half, 1), x) for x in values[j]]
                    higher_rows = [jnp.where(upper, x, pltpu.roll(x, LANES - half, 1)) for x in values[j]]
                else:
                    step = half // LANES
                    lower_rows = values[j & ~step]
                    higher_rows = values[j | step]
                moved = shifted(higher_rows, bits)
                after.append([x + y for x, y in zip(lower_rows, moved)])
            values = after
        for j in range(blocks):
            lanes = slice(j * LANES, (j + 1) * LANES)
            for t in range(samples):
                own_ref[t, b : b + 8, lanes] = values[j][t]
    send_ref[...] = own_ref[...].astype(jnp.bfloat16)


def tree(detected, shifts):
    return pl.pallas_call(
        tree_kernel,
        out_shape=[
            jax.ShapeDtypeStruct(detected.shape, jnp.float32),
            jax.ShapeDtypeStruct(detected.shape, jnp.bfloat16),
        ],
        compiler_params=pltpu.CompilerParams(vmem_limit_bytes=8 * MIB),
        name="tree",
    )(detected, shifts)


def merged(upper_ref, own_ref, partner_ref, shifts_ref, section, store):
    samples, beams, width = own_ref.shape
    upper = upper_ref[0] == 1
    for j in range(width // LANES):
        lanes = slice(j * LANES, (j + 1) * LANES)
        bits = digits(shifts_ref[section : section + 1, lanes], 8, (beams, LANES))
        own = [own_ref[t, :, lanes] for t in range(samples)]
        partner = [partner_ref[t, :, lanes].astype(jnp.float32) for t in range(samples)]
        lower_rows = [jnp.where(upper, y, x) for x, y in zip(own, partner)]
        higher_rows = [jnp.where(upper, x, y) for x, y in zip(own, partner)]
        moved = shifted(higher_rows, bits)
        for t in range(samples):
            store(t, lanes, lower_rows[t] + moved[t])


def merge_kernel(section, upper_ref, own_ref, partner_ref, shifts_ref, next_ref, send_ref):
    def store(t, lanes, value):
        next_ref[t, :, lanes] = value
        send_ref[t, :, lanes] = value.astype(jnp.bfloat16)

    merged(upper_ref, own_ref, partner_ref, shifts_ref, section, store)


def merge(section, upper, own, partner, shifts):
    return pl.pallas_call(
        functools.partial(merge_kernel, section),
        in_specs=[pl.BlockSpec(memory_space=pltpu.SMEM)] + [pl.BlockSpec(memory_space=pltpu.VMEM)] * 3,
        out_shape=[
            jax.ShapeDtypeStruct(own.shape, jnp.float32),
            jax.ShapeDtypeStruct(own.shape, jnp.bfloat16),
        ],
        compiler_params=pltpu.CompilerParams(vmem_limit_bytes=8 * MIB),
        name="merge",
    )(upper, own, partner, shifts)


def finish_kernel(section, upper_ref, widths_ref, own_ref, partner_ref, shifts_ref, series_ref, peaks_ref, sums, turned):
    samples, beams, width = own_ref.shape
    scale = 1.0 / (8.0 * math.sqrt(NSUB))

    def store(t, lanes, value):
        scaled = value * scale
        turned[lanes.start // LANES, pl.ds(t, beams, stride=samples), :] = scaled
        sums[t + 1, :, lanes] = scaled

    merged(upper_ref, own_ref, partner_ref, shifts_ref, section, store)
    for j in range(width // LANES):
        lanes = slice(j * LANES, (j + 1) * LANES)
        series_ref[:, :, lanes] = turned[j].reshape(beams, samples, LANES).astype(jnp.bfloat16)
    sums[0] = jnp.zeros((beams, width), jnp.float32)
    for t in range(2, samples + 1):
        sums[t] += sums[t - 1]
    for k in range(peaks_ref.shape[0]):
        reach = widths_ref[k]

        def widen(t, best):
            return jnp.maximum(best, sums[t + reach] - sums[t])

        best = lax.fori_loop(1, samples + 1 - reach, widen, sums[reach])
        peaks_ref[k] = best / jnp.sqrt(jnp.full((beams, width), reach).astype(jnp.float32))


def finish(section, upper, widths, own, partner, shifts):
    samples, beams, width = own.shape
    return pl.pallas_call(
        functools.partial(finish_kernel, section),
        in_specs=[pl.BlockSpec(memory_space=pltpu.SMEM)] * 2 + [pl.BlockSpec(memory_space=pltpu.VMEM)] * 3,
        out_shape=[
            jax.ShapeDtypeStruct((beams, samples, width), jnp.bfloat16),
            jax.ShapeDtypeStruct((widths.shape[0], beams, width), jnp.float32),
        ],
        scratch_shapes=[
            pltpu.VMEM((samples + 1, beams, width), jnp.float32),
            pltpu.VMEM((width // LANES, beams * samples, LANES), jnp.float32),
        ],
        compiler_params=pltpu.CompilerParams(vmem_limit_bytes=8 * MIB),
        name="finish",
    )(upper, widths, own, partner, shifts)


def swapped(block, axis, distance):
    count = lax.axis_size(axis)
    return lax.ppermute(block, axis, [(i, i ^ distance) for i in range(count)])


def shards(voltages, gains, shifts, widths):
    groups = lax.axis_size("beam")
    cross = lax.axis_size("freq").bit_length() - 1
    position = lax.axis_index("freq").astype(jnp.int32)
    matrix = steering(groups)
    calibrated = calibrate(voltages, gains)
    received = lax.all_to_all(calibrated, "beam", split_axis=0, concat_axis=0, tiled=True)
    detected = detect(received.reshape(2 * FEEDS, received.shape[2]), matrix)
    detected = detected.reshape(groups, FEEDS // groups, detected.shape[1])
    detected = lax.all_to_all(detected, "beam", split_axis=0, concat_axis=0, tiled=True)
    own, send = tree(detected, shifts)
    local = shifts.shape[1].bit_length() - 1
    for bit in range(cross):
        partner = swapped(send, "freq", 1 << bit)
        upper = (position >> bit & 1).reshape(1)
        if bit < cross - 1:
            own, send = merge(local + bit, upper, own, partner, shifts)
    return finish(local + cross - 1, upper, widths, own, partner, shifts)


def solution(mesh):
    return jax.shard_map(
        shards,
        mesh=mesh,
        in_specs=(P(None, "beam", None, "freq"), P(None, "beam", "freq"), P(None, "freq"), P()),
        out_specs=(P("beam", None, "freq"), P(None, "beam", "freq")),
        check_vma=False,
    )
```

```python
import functools
import math

import jax
import jax.numpy as jnp
from jax import lax
from jax.experimental import pallas as pl
from jax.experimental.pallas import tpu as pltpu
from jax.sharding import PartitionSpec as P

FEEDS = 256
CHAN_SUM = 4
NSUB = 4096
TIME = 16
LANES = 128
MIB = 1024 * 1024


def steering(groups):
    size = FEEDS // groups
    row = lax.broadcasted_iota(jnp.int32, (2 * FEEDS, 2 * FEEDS), 0)
    col = lax.broadcasted_iota(jnp.int32, (2 * FEEDS, 2 * FEEDS), 1)
    out_part = row // FEEDS
    beam = row % groups * size + row % FEEDS // groups
    feed = col // (2 * size) * size + col % size
    in_part = col // size % 2
    angles = (beam * feed % FEEDS).astype(jnp.float32) * (2.0 * math.pi / FEEDS)
    factor = 1.0 / math.sqrt(FEEDS)
    cosine = jnp.cos(angles) * factor
    sine = jnp.sin(angles) * factor
    value = jnp.where(in_part == out_part, cosine, jnp.where(out_part == 0, sine, -sine))
    return value.astype(jnp.bfloat16)


def calibrate_kernel(volt_ref, gain_ref, out_ref, scratch):
    feeds, samples, width = volt_ref.shape[1:]
    for j in range(width // LANES):
        lanes = slice(j * LANES, (j + 1) * LANES)
        for part in range(2):
            block = volt_ref[part, :, :, lanes].astype(jnp.float32)
            scratch[part, j] = block.reshape(feeds * samples, LANES)
        gain_re = gain_ref[0, :, lanes]
        gain_im = gain_ref[1, :, lanes]
        for t in range(samples):
            volt_re = scratch[0, j, pl.ds(t, feeds, stride=samples), :]
            volt_im = scratch[1, j, pl.ds(t, feeds, stride=samples), :]
            real = gain_re * volt_re - gain_im * volt_im
            imag = gain_re * volt_im + gain_im * volt_re
            out_ref[t, :feeds, lanes] = real.astype(jnp.bfloat16)
            out_ref[t, feeds:, lanes] = imag.astype(jnp.bfloat16)


def calibrate(voltages, gains):
    _, feeds, samples, width = voltages.shape
    step = 256
    return pl.pallas_call(
        calibrate_kernel,
        grid=(width // step,),
        in_specs=[
            pl.BlockSpec((2, feeds, samples, step), lambda i: (0, 0, 0, i)),
            pl.BlockSpec((2, feeds, step), lambda i: (0, 0, i)),
        ],
        out_specs=pl.BlockSpec((samples, 2 * feeds, step), lambda i: (0, 0, i)),
        out_shape=jax.ShapeDtypeStruct((samples, 2 * feeds, width), jnp.bfloat16),
        scratch_shapes=[pltpu.VMEM((2, step // LANES, feeds * samples, LANES), jnp.float32)],
        compiler_params=pltpu.CompilerParams(vmem_limit_bytes=60 * MIB),
        name="calibrate",
    )(voltages, gains)


def detect_kernel(matrix_ref, x_ref, out_ref, scratch):
    width = x_ref.shape[1]
    step = 256
    total = jnp.zeros((FEEDS, width // CHAN_SUM), jnp.float32)
    channel = lax.broadcasted_iota(jnp.int32, (step, width // CHAN_SUM), 0)
    group = lax.broadcasted_iota(jnp.int32, (step, width // CHAN_SUM), 1)
    for j in range(width // step):
        cols = slice(j * step, (j + 1) * step)
        formed = jnp.dot(matrix_ref[...], x_ref[:, cols], preferred_element_type=jnp.float32)
        power = formed[:FEEDS] * formed[:FEEDS] + formed[FEEDS:] * formed[FEEDS:]
        high = power.astype(jnp.bfloat16)
        low = (power - high.astype(jnp.float32)).astype(jnp.bfloat16)
        pooling = ((channel + j * step) // CHAN_SUM == group).astype(jnp.bfloat16)
        total += jnp.dot(high, pooling, preferred_element_type=jnp.float32)
        total += jnp.dot(low, pooling, preferred_element_type=jnp.float32)
    pieces = width // CHAN_SUM // LANES
    for h in range(pieces):
        scratch[pl.ds(h, FEEDS, stride=pieces), :] = total[:, h * LANES : (h + 1) * LANES]
    out_ref[...] = scratch[...].astype(jnp.bfloat16)


def detect(received, matrix):
    shape = (FEEDS * received.shape[1] // CHAN_SUM // LANES, LANES)
    return pl.pallas_call(
        detect_kernel,
        out_shape=jax.ShapeDtypeStruct(shape, jnp.bfloat16),
        scratch_shapes=[pltpu.VMEM(shape, jnp.float32)],
        compiler_params=pltpu.CompilerParams(vmem_limit_bytes=16 * MIB),
        name="detect",
    )(matrix, received)


def shifted(rows, bits):
    zero = jnp.zeros_like(rows[0])
    count = len(rows)
    for position, chosen in enumerate(bits):
        step = 1 << position
        rows = [jnp.where(chosen, rows[t + step] if t + step < count else zero, rows[t]) for t in range(count)]
    return rows


def digits(offsets, most):
    return [(offsets >> position & 1) == 1 for position in range(most.bit_length())]


def merged(lower_rows, higher_rows, bits):
    return [x + y for x, y in zip(lower_rows, shifted(higher_rows, bits))]


def folded(rows, axis, half, bits):
    size = rows[0].shape[axis]
    upper = (lax.broadcasted_iota(jnp.int32, rows[0].shape, axis) & half) != 0
    lower_rows = [jnp.where(upper, pltpu.roll(x, half, axis), x) for x in rows]
    higher_rows = [jnp.where(upper, x, pltpu.roll(x, size - half, axis)) for x in rows]
    return merged(lower_rows, higher_rows, bits)


def tree_kernel(detected_ref, shifts_ref, out_ref, wide, held, turned):
    blocks, samples, width = out_ref.shape
    pieces = width // LANES
    scale = 1.0 / (8.0 * math.sqrt(NSUB))
    wide[...] = detected_ref[...].astype(jnp.float32)

    def bits_of(section, group, piece):
        offsets = shifts_ref[section, group * 8 : (group + 1) * 8, piece * LANES : (piece + 1) * LANES]
        return digits(offsets, min(1 << section, 8))

    lane_bits = LANES.bit_length() - 1
    for group in range(blocks // 8):
        for piece in range(pieces):
            rows = []
            for t in range(samples):
                first = group * 8 * samples * pieces + t * pieces + piece
                rows.append(wide[pl.ds(first, 8, stride=samples * pieces), :])
            mean = functools.reduce(jnp.add, rows) * (1.0 / samples)
            rows = [row - mean for row in rows]
            for section in range(lane_bits):
                rows = folded(rows, 1, 1 << section, bits_of(section, group, piece))
            for t in range(samples):
                held[piece, group, t] = rows[t]
    for group in range(blocks // 8):
        for piece in range(pieces):
            lower_rows = [held[0, group, t] for t in range(samples)]
            higher_rows = [held[1, group, t] for t in range(samples)]
            rows = merged(lower_rows, higher_rows, bits_of(lane_bits, group, piece))
            for bit in range(3):
                section = lane_bits + 1 + bit
                rows = folded(rows, 0, 1 << bit, bits_of(section, group, piece))
            for t in range(samples):
                first = (group * pieces + piece) * samples * 8 + t * 8
                wide[first : first + 8, :] = rows[t]
    for piece in range(pieces):
        parts = []
        for group in range(2):
            first = (group * pieces + piece) * samples * 8
            parts.append([wide[first + t * 8 : first + t * 8 + 8, :] for t in range(samples)])
        for group in range(2):
            rows = merged(parts[0], parts[1], bits_of(lane_bits + 4, group, piece))
            for t in range(samples):
                turned[piece, pl.ds(group * 8 * samples + t, 8, stride=samples), :] = rows[t] * scale
        block = turned[piece].reshape(blocks, samples, LANES)
        out_ref[:, :, piece * LANES : (piece + 1) * LANES] = block.astype(jnp.bfloat16)


def tree(detected, shifts):
    sections, blocks, width = shifts.shape
    pieces = width // LANES
    rows = detected.shape[0]
    return pl.pallas_call(
        tree_kernel,
        out_shape=jax.ShapeDtypeStruct((blocks, TIME, width), jnp.bfloat16),
        scratch_shapes=[
            pltpu.VMEM((rows, LANES), jnp.float32),
            pltpu.VMEM((pieces, blocks // 8, TIME, 8, LANES), jnp.float32),
            pltpu.VMEM((pieces, blocks * TIME, LANES), jnp.float32),
        ],
        compiler_params=pltpu.CompilerParams(vmem_limit_bytes=8 * MIB),
        name="tree",
    )(detected, shifts)


def peaks_kernel(widths_ref, series_ref, same_ref, peaks_ref, wide, sums):
    beams, samples, width = series_ref.shape
    same_ref[...] = series_ref[...]
    for j in range(width // LANES):
        lanes = slice(j * LANES, (j + 1) * LANES)
        wide[j] = series_ref[:, :, lanes].astype(jnp.float32).reshape(beams * samples, LANES)
        total = jnp.zeros((beams, LANES), jnp.float32)
        sums[0, :, lanes] = total
        for t in range(samples):
            total = total + wide[j, pl.ds(t, beams, stride=samples), :]
            sums[t + 1, :, lanes] = total
    for k in range(peaks_ref.shape[0]):
        reach = widths_ref[k]

        def widen(t, best):
            return jnp.maximum(best, sums[t + reach] - sums[t])

        best = lax.fori_loop(1, samples + 1 - reach, widen, sums[reach])
        peaks_ref[k] = best / jnp.sqrt(jnp.full((beams, width), reach).astype(jnp.float32))


def peaks(widths, series):
    beams, samples, width = series.shape
    return pl.pallas_call(
        peaks_kernel,
        in_specs=[pl.BlockSpec(memory_space=pltpu.SMEM), pl.BlockSpec(memory_space=pltpu.VMEM)],
        out_shape=[
            jax.ShapeDtypeStruct(series.shape, series.dtype),
            jax.ShapeDtypeStruct((widths.shape[0], beams, width), jnp.float32),
        ],
        scratch_shapes=[
            pltpu.VMEM((width // LANES, beams * samples, LANES), jnp.float32),
            pltpu.VMEM((samples + 1, beams, width), jnp.float32),
        ],
        compiler_params=pltpu.CompilerParams(vmem_limit_bytes=8 * MIB),
        name="peaks",
    )(widths, series)


def gathered(block, axis):
    count = lax.axis_size(axis)
    position = lax.axis_index(axis)
    whole = block[None]
    for bit in range(count.bit_length() - 1):
        other = lax.ppermute(whole, axis, [(i, i ^ 1 << bit) for i in range(count)])
        upper = (position >> bit & 1) == 1
        whole = jnp.concatenate([jnp.where(upper, other, whole), jnp.where(upper, whole, other)])
    return whole


def exchanged(block, axes):
    return lax.all_to_all(block, axes, split_axis=0, concat_axis=0, tiled=True)


def shards(voltages, gains, shifts, widths):
    groups = lax.axis_size("beam")
    received = exchanged(calibrate(voltages, gains), "beam")
    table = jnp.transpose(gathered(shifts, "freq"), (1, 0, 2))
    early = (steering(groups), table, jnp.maximum(widths, 1))
    received, matrix, table, reach = lax.optimization_barrier((received, *early))
    detected = detect(received.reshape(2 * FEEDS, received.shape[2]), matrix)
    spread = exchanged(detected.reshape(FEEDS, -1, LANES), ("freq", "beam"))
    series = exchanged(tree(spread.reshape(detected.shape), table), "freq")
    return tuple(peaks(reach, series))


def solution(mesh):
    return jax.shard_map(
        shards,
        mesh=mesh,
        in_specs=(P(None, "beam", None, "freq"), P(None, "beam", "freq"), P(None, "freq"), P()),
        out_specs=(P("beam", None, "freq"), P(None, "beam", "freq")),
        check_vma=False,
    )
```

```python
import functools
import math

import jax
import jax.numpy as jnp
from jax import lax
from jax.experimental import pallas as pl
from jax.experimental.pallas import tpu as pltpu
from jax.sharding import PartitionSpec as P

FEEDS = 256
CHAN_SUM = 4
NSUB = 4096
TIME = 16
LANES = 128
CORES = 2
MIB = 1024 * 1024


def steering(groups):
    size = FEEDS // groups
    row = lax.broadcasted_iota(jnp.int32, (2 * FEEDS, 2 * FEEDS), 0)
    col = lax.broadcasted_iota(jnp.int32, (2 * FEEDS, 2 * FEEDS), 1)
    out_part = row // FEEDS
    beam = row % groups * size + row % FEEDS // groups
    feed = col // (2 * size) * size + col % size
    in_part = col // size % 2
    angles = (beam * feed % FEEDS).astype(jnp.float32) * (2.0 * math.pi / FEEDS)
    factor = 1.0 / math.sqrt(FEEDS)
    cosine = jnp.cos(angles) * factor
    sine = jnp.sin(angles) * factor
    value = jnp.where(in_part == out_part, cosine, jnp.where(out_part == 0, sine, -sine))
    return value.astype(jnp.bfloat16)


def calibrate_kernel(core_ref, volt_hbm, gain_hbm, *rest, other):
    out_hbm, volt, gain, wide, done, in_sems, out_sems = rest[-7:]
    chunks, _, feeds, samples, _ = volt.shape
    core = core_ref[0]
    slot = 1 - core if other else core

    def arriving(j):
        lanes = pl.ds(pl.multiple_of((core * chunks + j) * LANES, LANES), LANES)
        return (
            pltpu.make_async_copy(volt_hbm.at[:, :, :, lanes], volt.at[j], in_sems.at[0, j]),
            pltpu.make_async_copy(gain_hbm.at[:, :, lanes], gain.at[j], in_sems.at[1, j]),
        )

    def leaving(j):
        there = out_hbm.at[:, slot, :, pl.ds(j * LANES, LANES)]
        return pltpu.make_async_copy(done.at[j], there, out_sems.at[j])

    for j in range(chunks):
        for copy in arriving(j):
            copy.start()
    for j in range(chunks):
        for copy in arriving(j):
            copy.wait()
        for part in range(2):
            wide[j, part] = volt[j, part].astype(jnp.float32).reshape(feeds * samples, LANES)
        gain_re = gain[j, 0]
        gain_im = gain[j, 1]
        for t in range(samples):
            volt_re = wide[j, 0, pl.ds(t, feeds, stride=samples), :]
            volt_im = wide[j, 1, pl.ds(t, feeds, stride=samples), :]
            real = gain_re * volt_re - gain_im * volt_im
            imag = gain_re * volt_im + gain_im * volt_re
            done[j, t, :feeds] = real.astype(jnp.bfloat16)
            done[j, t, feeds:] = imag.astype(jnp.bfloat16)
        leaving(j).start()
    for j in range(chunks):
        leaving(j).wait()


def calibrate(core, voltages, gains, begun=None):
    _, feeds, samples, width = voltages.shape
    chunks = width // CORES // LANES
    shape = (samples, CORES, 2 * feeds, width // CORES)
    other = begun is not None
    operands = (core, voltages, gains) + ((begun,) if other else ())
    return pl.pallas_call(
        functools.partial(calibrate_kernel, other=other),
        in_specs=[pl.BlockSpec(memory_space=pltpu.SMEM)]
        + [pl.BlockSpec(memory_space=pl.ANY if other else pltpu.HBM)] * 2
        + [pl.BlockSpec(memory_space=pltpu.HBM)] * other,
        out_specs=pl.BlockSpec(memory_space=pltpu.HBM),
        out_shape=jax.ShapeDtypeStruct(shape, jnp.bfloat16),
        scratch_shapes=[
            pltpu.VMEM((chunks, 2, feeds, samples, LANES), jnp.bfloat16),
            pltpu.VMEM((chunks, 2, feeds, LANES), jnp.float32),
            pltpu.VMEM((chunks, 2, feeds * samples, LANES), jnp.float32),
            pltpu.VMEM((chunks, samples, 2 * feeds, LANES), jnp.bfloat16),
            pltpu.SemaphoreType.DMA((2, chunks)),
            pltpu.SemaphoreType.DMA((chunks,)),
        ],
        input_output_aliases={3: 0} if other else {},
        compiler_params=pltpu.CompilerParams(vmem_limit_bytes=(8 if other else 60) * MIB),
        name="calibrate",
    )(*operands)


def detect_kernel(matrix_ref, x_ref, out_ref, scratch):
    _, pair, _, _, width = x_ref.shape
    step = 256
    channel = lax.broadcasted_iota(jnp.int32, (step, width // CHAN_SUM), 0)
    group = lax.broadcasted_iota(jnp.int32, (step, width // CHAN_SUM), 1)
    for t in range(pair):
        total = jnp.zeros((FEEDS, width // CHAN_SUM), jnp.float32)
        for j in range(width // step):
            x = x_ref[:, t, :, :, j * step : (j + 1) * step].reshape(2 * FEEDS, step)
            formed = jnp.dot(matrix_ref[...], x, preferred_element_type=jnp.float32)
            power = formed[:FEEDS] * formed[:FEEDS] + formed[FEEDS:] * formed[FEEDS:]
            high = power.astype(jnp.bfloat16)
            low = (power - high.astype(jnp.float32)).astype(jnp.bfloat16)
            pooling = ((channel + j * step) // CHAN_SUM == group).astype(jnp.bfloat16)
            total += jnp.dot(high, pooling, preferred_element_type=jnp.float32)
            total += jnp.dot(low, pooling, preferred_element_type=jnp.float32)
        scratch[pl.ds(t, FEEDS, stride=pair), :] = total
    out_ref[...] = scratch[...].astype(jnp.bfloat16)


def detect(received, matrix):
    shape = (FEEDS * received.shape[1], received.shape[4] // CHAN_SUM)
    return pl.pallas_call(
        detect_kernel,
        out_shape=jax.ShapeDtypeStruct(shape, jnp.bfloat16),
        scratch_shapes=[pltpu.VMEM(shape, jnp.float32)],
        compiler_params=pltpu.CompilerParams(vmem_limit_bytes=16 * MIB),
        name="detect",
    )(matrix, received)


def shifted(rows, bits):
    zero = jnp.zeros_like(rows[0])
    count = len(rows)
    for position, chosen in enumerate(bits):
        step = 1 << position
        rows = [jnp.where(chosen, rows[t + step] if t + step < count else zero, rows[t]) for t in range(count)]
    return rows


def digits(offsets, most):
    return [(offsets >> position & 1) == 1 for position in range(most.bit_length())]


def merged(lower_rows, higher_rows, bits):
    return [x + y for x, y in zip(lower_rows, shifted(higher_rows, bits))]


def folded(rows, axis, half, bits):
    size = rows[0].shape[axis]
    upper = (lax.broadcasted_iota(jnp.int32, rows[0].shape, axis) & half) != 0
    lower_rows = [jnp.where(upper, pltpu.roll(x, half, axis), x) for x in rows]
    higher_rows = [jnp.where(upper, x, pltpu.roll(x, size - half, axis)) for x in rows]
    return merged(lower_rows, higher_rows, bits)


def tree_kernel(detected_ref, shifts_ref, out_ref, wide, held, turned):
    blocks, samples, width = out_ref.shape
    pieces = width // LANES
    scale = 1.0 / (8.0 * math.sqrt(NSUB))
    wide[...] = detected_ref[...].astype(jnp.float32)

    def bits_of(section, group, piece):
        offsets = shifts_ref[section, group * 8 : (group + 1) * 8, piece * LANES : (piece + 1) * LANES]
        return digits(offsets, min(1 << section, 8))

    lane_bits = LANES.bit_length() - 1
    for group in range(blocks // 8):
        for piece in range(pieces):
            rows = []
            for t in range(samples):
                first = (group * 8 * samples + t // 2 * 2 + piece) * pieces + t % 2
                rows.append(wide[pl.ds(first, 8, stride=samples * pieces), :])
            mean = functools.reduce(jnp.add, rows) * (1.0 / samples)
            rows = [row - mean for row in rows]
            for section in range(lane_bits):
                rows = folded(rows, 1, 1 << section, bits_of(section, group, piece))
            for t in range(samples):
                held[piece, group, t] = rows[t]
    for group in range(blocks // 8):
        for piece in range(pieces):
            lower_rows = [held[0, group, t] for t in range(samples)]
            higher_rows = [held[1, group, t] for t in range(samples)]
            rows = merged(lower_rows, higher_rows, bits_of(lane_bits, group, piece))
            for bit in range(3):
                section = lane_bits + 1 + bit
                rows = folded(rows, 0, 1 << bit, bits_of(section, group, piece))
            for t in range(samples):
                first = (group * pieces + piece) * samples * 8 + t * 8
                wide[first : first + 8, :] = rows[t]
    for piece in range(pieces):
        parts = []
        for group in range(2):
            first = (group * pieces + piece) * samples * 8
            parts.append([wide[first + t * 8 : first + t * 8 + 8, :] for t in range(samples)])
        for group in range(2):
            rows = merged(parts[0], parts[1], bits_of(lane_bits + 4, group, piece))
            for t in range(samples):
                turned[piece, pl.ds(group * 8 * samples + t, 8, stride=samples), :] = rows[t] * scale
        block = turned[piece].reshape(blocks, samples, LANES)
        out_ref[:, :, piece * LANES : (piece + 1) * LANES] = block.astype(jnp.bfloat16)


def tree(detected, shifts):
    sections, blocks, width = shifts.shape
    pieces = width // LANES
    rows = detected.shape[0]
    return pl.pallas_call(
        tree_kernel,
        out_shape=jax.ShapeDtypeStruct((blocks, TIME, width), jnp.bfloat16),
        scratch_shapes=[
            pltpu.VMEM((rows, LANES), jnp.float32),
            pltpu.VMEM((pieces, blocks // 8, TIME, 8, LANES), jnp.float32),
            pltpu.VMEM((pieces, blocks * TIME, LANES), jnp.float32),
        ],
        compiler_params=pltpu.CompilerParams(vmem_limit_bytes=8 * MIB),
        name="tree",
    )(detected, shifts)


def peaks_kernel(widths_ref, series_ref, same_ref, peaks_ref, wide, sums):
    beams, samples, width = series_ref.shape
    same_ref[...] = series_ref[...]
    for j in range(width // LANES):
        lanes = slice(j * LANES, (j + 1) * LANES)
        wide[j] = series_ref[:, :, lanes].astype(jnp.float32).reshape(beams * samples, LANES)
        total = jnp.zeros((beams, LANES), jnp.float32)
        sums[0, :, lanes] = total
        for t in range(samples):
            total = total + wide[j, pl.ds(t, beams, stride=samples), :]
            sums[t + 1, :, lanes] = total
    for k in range(peaks_ref.shape[0]):
        reach = widths_ref[k]

        def widen(t, best):
            return jnp.maximum(best, sums[t + reach] - sums[t])

        best = lax.fori_loop(1, samples + 1 - reach, widen, sums[reach])
        peaks_ref[k] = best / jnp.sqrt(jnp.full((beams, width), reach).astype(jnp.float32))


def peaks(widths, series):
    beams, samples, width = series.shape
    return pl.pallas_call(
        peaks_kernel,
        in_specs=[pl.BlockSpec(memory_space=pltpu.SMEM), pl.BlockSpec(memory_space=pltpu.VMEM)],
        out_shape=[
            jax.ShapeDtypeStruct(series.shape, series.dtype),
            jax.ShapeDtypeStruct((widths.shape[0], beams, width), jnp.float32),
        ],
        scratch_shapes=[
            pltpu.VMEM((width // LANES, beams * samples, LANES), jnp.float32),
            pltpu.VMEM((samples + 1, beams, width), jnp.float32),
        ],
        compiler_params=pltpu.CompilerParams(vmem_limit_bytes=8 * MIB),
        name="peaks",
    )(widths, series)


def gathered(block, axis):
    count = lax.axis_size(axis)
    position = lax.axis_index(axis)
    whole = block[None]
    step = 1
    while step < count:
        parts = [whole]
        for k in range(1, 4):
            parts.append(lax.ppermute(whole, axis, [(i, i ^ k * step) for i in range(count)]))
        for bit in (1, 2):
            odd = position & bit * step != 0
            parts = [jnp.where(odd, parts[k ^ bit], parts[k]) for k in range(4)]
        whole = jnp.concatenate(parts)
        step *= 4
    return whole


def exchanged(block, axes, groups=None):
    return lax.all_to_all(block, axes, split_axis=0, concat_axis=0, axis_index_groups=groups, tiled=True)


def shards(voltages, gains, shifts, widths):
    groups = lax.axis_size("beam")
    core = (lax.axis_index("beam") & CORES - 1).astype(jnp.int32).reshape(1)
    swap = [(i, i ^ 1) for i in range(groups)]
    other = [lax.ppermute(block, "beam", swap) for block in (voltages, gains)]
    calibrated = calibrate(core, *other, calibrate(core, voltages, gains))
    calibrated, shifts = lax.optimization_barrier((calibrated, shifts))
    same_core = [list(range(c, groups, CORES)) for c in range(CORES)]
    received = exchanged(calibrated, "beam", same_core)
    received = received.reshape((groups // CORES, CORES) + calibrated.shape[1:])
    table = jnp.transpose(gathered(shifts, "freq"), (1, 0, 2))
    early = (steering(groups), table, jnp.maximum(widths, 1))
    received, matrix, table, reach = lax.optimization_barrier((received, *early))
    detected = detect(received, matrix)
    spread = exchanged(detected.reshape(FEEDS, -1, LANES), ("freq", "beam"))
    series = exchanged(tree(spread.reshape(detected.shape), table), "freq")
    return tuple(peaks(reach, series))


def solution(mesh):
    return jax.shard_map(
        shards,
        mesh=mesh,
        in_specs=(P(None, "beam", None, "freq"), P(None, "beam", "freq"), P(None, "freq"), P()),
        out_specs=(P("beam", None, "freq"), P(None, "beam", "freq")),
        check_vma=False,
    )
```

```python
import functools
import math

import jax
import jax.numpy as jnp
from jax import lax
from jax.experimental import pallas as pl
from jax.experimental.pallas import tpu as pltpu
from jax.sharding import PartitionSpec as P

FEEDS = 256
CHAN_SUM = 4
NSUB = 4096
TIME = 16
LANES = 128
MIB = 1024 * 1024


def steering(groups):
    size = FEEDS // groups
    row = lax.broadcasted_iota(jnp.int32, (2 * FEEDS, 2 * FEEDS), 0)
    col = lax.broadcasted_iota(jnp.int32, (2 * FEEDS, 2 * FEEDS), 1)
    out_part = row // FEEDS
    beam = row % groups * size + row % FEEDS // groups
    feed = col // (2 * size) * size + col % size
    in_part = col // size % 2
    angles = (beam * feed % FEEDS).astype(jnp.float32) * (2.0 * math.pi / FEEDS)
    factor = 1.0 / math.sqrt(FEEDS)
    cosine = jnp.cos(angles) * factor
    sine = jnp.sin(angles) * factor
    value = jnp.where(in_part == out_part, cosine, jnp.where(out_part == 0, sine, -sine))
    return value.astype(jnp.bfloat16)


def calibrate_kernel(volt_hbm, gain_hbm, out_hbm, volt, gain, wide, done, in_sems, out_sems):
    chunks, _, feeds, samples, _ = volt.shape

    def arriving(j):
        lanes = pl.ds(j * LANES, LANES)
        return (
            pltpu.make_async_copy(volt_hbm.at[:, :, :, lanes], volt.at[j], in_sems.at[0, j]),
            pltpu.make_async_copy(gain_hbm.at[:, :, lanes], gain.at[j], in_sems.at[1, j]),
        )

    def leaving(j):
        return pltpu.make_async_copy(done.at[j], out_hbm.at[:, :, pl.ds(j * LANES, LANES)], out_sems.at[j])

    for j in range(chunks):
        for copy in arriving(j):
            copy.start()
    for j in range(chunks):
        for copy in arriving(j):
            copy.wait()
        for part in range(2):
            wide[j, part] = volt[j, part].astype(jnp.float32).reshape(feeds * samples, LANES)
        gain_re = gain[j, 0]
        gain_im = gain[j, 1]
        for t in range(samples):
            volt_re = wide[j, 0, pl.ds(t, feeds, stride=samples), :]
            volt_im = wide[j, 1, pl.ds(t, feeds, stride=samples), :]
            real = gain_re * volt_re - gain_im * volt_im
            imag = gain_re * volt_im + gain_im * volt_re
            done[j, t, :feeds] = real.astype(jnp.bfloat16)
            done[j, t, feeds:] = imag.astype(jnp.bfloat16)
        leaving(j).start()
    for j in range(chunks):
        leaving(j).wait()


def calibrate(voltages, gains):
    _, feeds, samples, width = voltages.shape
    chunks = width // LANES
    return pl.pallas_call(
        calibrate_kernel,
        in_specs=[pl.BlockSpec(memory_space=pl.ANY)] * 2,
        out_specs=pl.BlockSpec(memory_space=pltpu.HBM),
        out_shape=jax.ShapeDtypeStruct((samples, 2 * feeds, width), jnp.bfloat16),
        scratch_shapes=[
            pltpu.VMEM((chunks, 2, feeds, samples, LANES), jnp.bfloat16),
            pltpu.VMEM((chunks, 2, feeds, LANES), jnp.float32),
            pltpu.VMEM((chunks, 2, feeds * samples, LANES), jnp.float32),
            pltpu.VMEM((chunks, samples, 2 * feeds, LANES), jnp.bfloat16),
            pltpu.SemaphoreType.DMA((2, chunks)),
            pltpu.SemaphoreType.DMA((chunks,)),
        ],
        compiler_params=pltpu.CompilerParams(vmem_limit_bytes=60 * MIB),
        name="calibrate",
    )(voltages, gains)


def detect_kernel(matrix_ref, x_ref, out_ref, scratch):
    width = x_ref.shape[1]
    step = 256
    total = jnp.zeros((FEEDS, width // CHAN_SUM), jnp.float32)
    channel = lax.broadcasted_iota(jnp.int32, (step, width // CHAN_SUM), 0)
    group = lax.broadcasted_iota(jnp.int32, (step, width // CHAN_SUM), 1)
    for j in range(width // step):
        cols = slice(j * step, (j + 1) * step)
        formed = jnp.dot(matrix_ref[...], x_ref[:, cols], preferred_element_type=jnp.float32)
        power = formed[:FEEDS] * formed[:FEEDS] + formed[FEEDS:] * formed[FEEDS:]
        pooling = ((channel + j * step) // CHAN_SUM == group).astype(jnp.bfloat16)
        total += jnp.dot(power.astype(jnp.bfloat16), pooling, preferred_element_type=jnp.float32)
    pieces = width // CHAN_SUM // LANES
    for h in range(pieces):
        scratch[pl.ds(h, FEEDS, stride=pieces), :] = total[:, h * LANES : (h + 1) * LANES]
    out_ref[...] = scratch[...].astype(jnp.bfloat16)


def detect(received, matrix):
    shape = (FEEDS * received.shape[1] // CHAN_SUM // LANES, LANES)
    return pl.pallas_call(
        detect_kernel,
        out_shape=jax.ShapeDtypeStruct(shape, jnp.bfloat16),
        scratch_shapes=[pltpu.VMEM(shape, jnp.float32)],
        compiler_params=pltpu.CompilerParams(vmem_limit_bytes=16 * MIB),
        name="detect",
    )(matrix, received)


def shifted(rows, bits):
    zero = jnp.zeros_like(rows[0])
    count = len(rows)
    for position, chosen in enumerate(bits):
        step = 1 << position
        rows = [jnp.where(chosen, rows[t + step] if t + step < count else zero, rows[t]) for t in range(count)]
    return rows


def digits(offsets, most):
    return [(offsets >> position & 1) == 1 for position in range(most.bit_length())]


def merged(lower_rows, higher_rows, bits):
    return [x + y for x, y in zip(lower_rows, shifted(higher_rows, bits))]


def folded(rows, axis, half, bits):
    size = rows[0].shape[axis]
    upper = (lax.broadcasted_iota(jnp.int32, rows[0].shape, axis) & half) != 0
    lower_rows = [jnp.where(upper, pltpu.roll(x, half, axis), x) for x in rows]
    higher_rows = [jnp.where(upper, x, pltpu.roll(x, size - half, axis)) for x in rows]
    return merged(lower_rows, higher_rows, bits)


def tree_kernel(detected_ref, shifts_ref, out_ref, wide, held, turned):
    blocks, samples, width = out_ref.shape
    pieces = width // LANES
    scale = 1.0 / (8.0 * math.sqrt(NSUB))
    wide[...] = detected_ref[...].astype(jnp.float32)

    def bits_of(section, group, piece):
        offsets = shifts_ref[section, group * 8 : (group + 1) * 8, piece * LANES : (piece + 1) * LANES]
        return digits(offsets, min(1 << section, 8))

    lane_bits = LANES.bit_length() - 1
    for group in range(blocks // 8):
        for piece in range(pieces):
            rows = []
            for t in range(samples):
                first = group * 8 * samples * pieces + t * pieces + piece
                rows.append(wide[pl.ds(first, 8, stride=samples * pieces), :])
            mean = functools.reduce(jnp.add, rows) * (1.0 / samples)
            rows = [row - mean for row in rows]
            for section in range(lane_bits):
                rows = folded(rows, 1, 1 << section, bits_of(section, group, piece))
            for t in range(samples):
                held[piece, group, t] = rows[t]
    for group in range(blocks // 8):
        for piece in range(pieces):
            lower_rows = [held[0, group, t] for t in range(samples)]
            higher_rows = [held[1, group, t] for t in range(samples)]
            rows = merged(lower_rows, higher_rows, bits_of(lane_bits, group, piece))
            for bit in range(3):
                section = lane_bits + 1 + bit
                rows = folded(rows, 0, 1 << bit, bits_of(section, group, piece))
            for t in range(samples):
                first = (group * pieces + piece) * samples * 8 + t * 8
                wide[first : first + 8, :] = rows[t]
    for piece in range(pieces):
        parts = []
        for group in range(2):
            first = (group * pieces + piece) * samples * 8
            parts.append([wide[first + t * 8 : first + t * 8 + 8, :] for t in range(samples)])
        for group in range(2):
            rows = merged(parts[0], parts[1], bits_of(lane_bits + 4, group, piece))
            for t in range(samples):
                turned[piece, pl.ds(group * 8 * samples + t, 8, stride=samples), :] = rows[t] * scale
        block = turned[piece].reshape(blocks, samples, LANES)
        out_ref[:, :, piece * LANES : (piece + 1) * LANES] = block.astype(jnp.bfloat16)


def tree(detected, shifts):
    sections, blocks, width = shifts.shape
    pieces = width // LANES
    rows = detected.shape[0]
    return pl.pallas_call(
        tree_kernel,
        out_shape=jax.ShapeDtypeStruct((blocks, TIME, width), jnp.bfloat16),
        scratch_shapes=[
            pltpu.VMEM((rows, LANES), jnp.float32),
            pltpu.VMEM((pieces, blocks // 8, TIME, 8, LANES), jnp.float32),
            pltpu.VMEM((pieces, blocks * TIME, LANES), jnp.float32),
        ],
        compiler_params=pltpu.CompilerParams(vmem_limit_bytes=8 * MIB),
        name="tree",
    )(detected, shifts)


def width_range(k):
    return (min(2 ** (k - 1) + 1, TIME), min(2**k, TIME)) if k else (1, 1)


def peaks_kernel(widths_ref, series_ref, same_hbm, peaks_hbm, wide, sums, best, same_sem, sems):
    beams, samples, width = series_ref.shape
    same = pltpu.make_async_copy(series_ref, same_hbm, same_sem)
    same.start()
    for j in range(width // LANES):
        lanes = slice(j * LANES, (j + 1) * LANES)
        wide[j] = series_ref[:, :, lanes].astype(jnp.float32).reshape(beams * samples, LANES)
        total = jnp.zeros((beams, LANES), jnp.float32)
        sums[0, :, lanes] = total
        for t in range(samples):
            total = total + wide[j, pl.ds(t, beams, stride=samples), :]
            sums[t + 1, :, lanes] = total
    for t in range(samples + 1, sums.shape[0]):
        sums[t] = jnp.full((beams, width), -1e30, jnp.float32)
    copies = []
    for k in range(best.shape[0]):
        reach = widths_ref[k]
        value = sums[reach]
        for t in range(1, samples + 1 - width_range(k)[0]):
            value = jnp.maximum(value, sums[t + reach] - sums[t])
        best[k] = value / jnp.sqrt(jnp.full((beams, width), reach).astype(jnp.float32))
        copies.append(pltpu.make_async_copy(best.at[k], peaks_hbm.at[k], sems.at[k]))
        copies[-1].start()
    same.wait()
    for copy in copies:
        copy.wait()


def peaks(widths, series):
    beams, samples, width = series.shape
    count = widths.shape[0]
    rows = max(samples + 1 - low + high for low, high in map(width_range, range(count)))
    return pl.pallas_call(
        peaks_kernel,
        in_specs=[pl.BlockSpec(memory_space=pltpu.SMEM), pl.BlockSpec(memory_space=pltpu.VMEM)],
        out_specs=[pl.BlockSpec(memory_space=pltpu.HBM)] * 2,
        out_shape=[
            jax.ShapeDtypeStruct(series.shape, series.dtype),
            jax.ShapeDtypeStruct((count, beams, width), jnp.float32),
        ],
        scratch_shapes=[
            pltpu.VMEM((width // LANES, beams * samples, LANES), jnp.float32),
            pltpu.VMEM((rows, beams, width), jnp.float32),
            pltpu.VMEM((count, beams, width), jnp.float32),
            pltpu.SemaphoreType.DMA,
            pltpu.SemaphoreType.DMA((count,)),
        ],
        compiler_params=pltpu.CompilerParams(vmem_limit_bytes=8 * MIB),
        name="peaks",
    )(widths, series)


def gathered(block, axis):
    count = lax.axis_size(axis)
    position = lax.axis_index(axis)
    whole = block[None]
    step = 1
    while step < count:
        parts = [whole]
        for k in range(1, 4):
            parts.append(lax.ppermute(whole, axis, [(i, i ^ k * step) for i in range(count)]))
        for bit in (1, 2):
            odd = position & bit * step != 0
            parts = [jnp.where(odd, parts[k ^ bit], parts[k]) for k in range(4)]
        whole = jnp.concatenate(parts)
        step *= 4
    return whole


def exchanged(block, axes):
    return lax.all_to_all(block, axes, split_axis=0, concat_axis=0, tiled=True)


def shards(voltages, gains, shifts, widths):
    groups = lax.axis_size("beam")
    received = exchanged(calibrate(voltages, gains), "beam")
    matrix, shifts = lax.optimization_barrier((steering(groups), shifts))
    table = jnp.transpose(gathered(shifts, "freq"), (1, 0, 2))
    early = (matrix, table, jnp.maximum(widths, 1))
    received, matrix, table, reach = lax.optimization_barrier((received, *early))
    detected = detect(received.reshape(2 * FEEDS, received.shape[2]), matrix)
    spread = exchanged(detected.reshape(FEEDS, -1, LANES), ("freq", "beam"))
    series = exchanged(tree(spread.reshape(detected.shape), table), "freq")
    return tuple(peaks(reach, series))


def solution(mesh):
    return jax.shard_map(
        shards,
        mesh=mesh,
        in_specs=(P(None, "beam", None, "freq"), P(None, "beam", "freq"), P(None, "freq"), P()),
        out_specs=(P("beam", None, "freq"), P(None, "beam", "freq")),
        check_vma=False,
    )
```

```python
import functools
import math

import jax
import jax.numpy as jnp
from jax import lax
from jax.experimental import pallas as pl
from jax.experimental.pallas import tpu as pltpu
from jax.sharding import PartitionSpec as P

FEEDS = 256
CHAN_SUM = 4
NSUB = 4096
TIME = 16
LANES = 128
PITCH = 24
MIB = 1024 * 1024


def steering(groups):
    size = FEEDS // groups
    row = lax.broadcasted_iota(jnp.int32, (2 * FEEDS, 2 * FEEDS), 0)
    col = lax.broadcasted_iota(jnp.int32, (2 * FEEDS, 2 * FEEDS), 1)
    out_part = row // FEEDS
    beam = row % groups * size + row % FEEDS // groups
    feed = col // (2 * size) * size + col % size
    in_part = col // size % 2
    angles = (beam * feed % FEEDS).astype(jnp.float32) * (2.0 * math.pi / FEEDS)
    factor = 1.0 / math.sqrt(FEEDS)
    cosine = jnp.cos(angles) * factor
    sine = jnp.sin(angles) * factor
    value = jnp.where(in_part == out_part, cosine, jnp.where(out_part == 0, sine, -sine))
    return value.astype(jnp.bfloat16)


def calibrate_kernel(volt_hbm, gain_hbm, out_hbm, volt, gain, wide, done, in_sems, out_sems):
    chunks, _, feeds, samples, _ = volt.shape

    def arriving(j):
        lanes = pl.ds(j * LANES, LANES)
        return (
            pltpu.make_async_copy(volt_hbm.at[:, :, :, lanes], volt.at[j], in_sems.at[0, j]),
            pltpu.make_async_copy(gain_hbm.at[:, :, lanes], gain.at[j], in_sems.at[1, j]),
        )

    def leaving(j):
        return pltpu.make_async_copy(done.at[j], out_hbm.at[:, :, pl.ds(j * LANES, LANES)], out_sems.at[j])

    for j in range(chunks):
        for copy in arriving(j):
            copy.start()
    for j in range(chunks):
        for copy in arriving(j):
            copy.wait()
        for part in range(2):
            block = volt[j, part].astype(jnp.float32)
            for f in range(feeds):
                wide[j, part, f * PITCH : f * PITCH + samples] = block[f]
        gain_re = gain[j, 0]
        gain_im = gain[j, 1]
        for t in range(samples):
            volt_re = wide[j, 0, pl.ds(t, feeds, stride=PITCH), :]
            volt_im = wide[j, 1, pl.ds(t, feeds, stride=PITCH), :]
            real = gain_re * volt_re - gain_im * volt_im
            imag = gain_re * volt_im + gain_im * volt_re
            done[j, t, :feeds] = real.astype(jnp.bfloat16)
            done[j, t, feeds:] = imag.astype(jnp.bfloat16)
        leaving(j).start()
    for j in range(chunks):
        leaving(j).wait()


def calibrate(voltages, gains):
    _, feeds, samples, width = voltages.shape
    chunks = width // LANES
    return pl.pallas_call(
        calibrate_kernel,
        in_specs=[pl.BlockSpec(memory_space=pl.ANY)] * 2,
        out_specs=pl.BlockSpec(memory_space=pltpu.HBM),
        out_shape=jax.ShapeDtypeStruct((samples, 2 * feeds, width), jnp.bfloat16),
        scratch_shapes=[
            pltpu.VMEM((chunks, 2, feeds, samples, LANES), jnp.bfloat16),
            pltpu.VMEM((chunks, 2, feeds, LANES), jnp.float32),
            pltpu.VMEM((chunks, 2, feeds * PITCH, LANES), jnp.float32),
            pltpu.VMEM((chunks, samples, 2 * feeds, LANES), jnp.bfloat16),
            pltpu.SemaphoreType.DMA((2, chunks)),
            pltpu.SemaphoreType.DMA((chunks,)),
        ],
        compiler_params=pltpu.CompilerParams(vmem_limit_bytes=60 * MIB),
        name="calibrate",
    )(voltages, gains)


def detect_kernel(matrix_ref, x_ref, out_ref, scratch):
    width = x_ref.shape[1]
    step = 256
    total = jnp.zeros((FEEDS, width // CHAN_SUM), jnp.float32)
    channel = lax.broadcasted_iota(jnp.int32, (step, width // CHAN_SUM), 0)
    group = lax.broadcasted_iota(jnp.int32, (step, width // CHAN_SUM), 1)
    for j in range(width // step):
        cols = slice(j * step, (j + 1) * step)
        formed = jnp.dot(matrix_ref[...], x_ref[:, cols], preferred_element_type=jnp.float32)
        power = formed[:FEEDS] * formed[:FEEDS] + formed[FEEDS:] * formed[FEEDS:]
        sums = []
        for lane in range(0, step, LANES):
            part = power[:, lane : lane + LANES]
            part = part + pltpu.roll(part, LANES - 1, 1)
            sums.append(part + pltpu.roll(part, LANES - 2, 1))
        picking = (channel + j * step == group * CHAN_SUM).astype(jnp.bfloat16)
        summed = jnp.concatenate(sums, axis=1).astype(jnp.bfloat16)
        total += jnp.dot(summed, picking, preferred_element_type=jnp.float32)
    pieces = width // CHAN_SUM // LANES
    for h in range(pieces):
        scratch[pl.ds(h, FEEDS, stride=pieces), :] = total[:, h * LANES : (h + 1) * LANES]
    out_ref[...] = scratch[...].astype(jnp.bfloat16)


def detect(received, matrix):
    shape = (FEEDS * received.shape[1] // CHAN_SUM // LANES, LANES)
    return pl.pallas_call(
        detect_kernel,
        out_shape=jax.ShapeDtypeStruct(shape, jnp.bfloat16),
        scratch_shapes=[pltpu.VMEM(shape, jnp.float32)],
        compiler_params=pltpu.CompilerParams(vmem_limit_bytes=16 * MIB),
        name="detect",
    )(matrix, received)


def shifted(rows, bits):
    zero = jnp.zeros_like(rows[0])
    count = len(rows)
    for position, chosen in enumerate(bits):
        step = 1 << position
        rows = [jnp.where(chosen, rows[t + step] if t + step < count else zero, rows[t]) for t in range(count)]
    return rows


def digits(offsets, most):
    return [(offsets >> position & 1) == 1 for position in range(most.bit_length())]


def merged(lower_rows, higher_rows, bits):
    return [x + y for x, y in zip(lower_rows, shifted(higher_rows, bits))]


def folded(rows, axis, half, bits):
    place = lax.broadcasted_iota(jnp.int32, rows[0].shape, axis)
    upper = (place & half) != 0
    facing = [jnp.take_along_axis(x, place ^ half, axis=axis) for x in rows]
    lower_rows = [jnp.where(upper, y, x) for x, y in zip(rows, facing)]
    higher_rows = [jnp.where(upper, x, y) for x, y in zip(rows, facing)]
    return merged(lower_rows, higher_rows, bits)


def tree_kernel(detected_ref, shifts_ref, out_ref, wide, held, turned):
    blocks, samples, width = out_ref.shape
    pieces = width // LANES
    scale = 1.0 / (8.0 * math.sqrt(NSUB))
    wide[...] = detected_ref[...].astype(jnp.float32)

    def bits_of(section, group, piece):
        offsets = shifts_ref[section, group * 8 : (group + 1) * 8, piece * LANES : (piece + 1) * LANES]
        return digits(offsets, min(1 << section, 8))

    lane_bits = LANES.bit_length() - 1
    for group in range(blocks // 8):
        for piece in range(pieces):
            rows = []
            for t in range(samples):
                first = group * 8 * samples * pieces + t * pieces + piece
                rows.append(wide[pl.ds(first, 8, stride=samples * pieces), :])
            mean = functools.reduce(jnp.add, rows) * (1.0 / samples)
            rows = [row - mean for row in rows]
            for section in range(lane_bits):
                rows = folded(rows, 1, 1 << section, bits_of(section, group, piece))
            for t in range(samples):
                held[piece, group, t] = rows[t]
    for group in range(blocks // 8):
        for piece in range(pieces):
            lower_rows = [held[0, group, t] for t in range(samples)]
            higher_rows = [held[1, group, t] for t in range(samples)]
            rows = merged(lower_rows, higher_rows, bits_of(lane_bits, group, piece))
            for bit in range(3):
                section = lane_bits + 1 + bit
                rows = folded(rows, 0, 1 << bit, bits_of(section, group, piece))
            for t in range(samples):
                first = (group * pieces + piece) * samples * 8 + t * 8
                wide[first : first + 8, :] = rows[t]
    for piece in range(pieces):
        parts = []
        for group in range(2):
            first = (group * pieces + piece) * samples * 8
            parts.append([wide[first + t * 8 : first + t * 8 + 8, :] for t in range(samples)])
        for group in range(2):
            rows = merged(parts[0], parts[1], bits_of(lane_bits + 4, group, piece))
            for t in range(samples):
                turned[piece, pl.ds(group * 8 * samples + t, 8, stride=samples), :] = rows[t] * scale
        block = turned[piece].reshape(blocks, samples, LANES)
        out_ref[:, :, piece * LANES : (piece + 1) * LANES] = block.astype(jnp.bfloat16)


def tree(detected, shifts):
    sections, blocks, width = shifts.shape
    pieces = width // LANES
    rows = detected.shape[0]
    return pl.pallas_call(
        tree_kernel,
        out_shape=jax.ShapeDtypeStruct((blocks, TIME, width), jnp.bfloat16),
        scratch_shapes=[
            pltpu.VMEM((rows, LANES), jnp.float32),
            pltpu.VMEM((pieces, blocks // 8, TIME, 8, LANES), jnp.float32),
            pltpu.VMEM((pieces, blocks * TIME, LANES), jnp.float32),
        ],
        compiler_params=pltpu.CompilerParams(vmem_limit_bytes=8 * MIB),
        name="tree",
    )(detected, shifts)


def width_range(k):
    return (min(2 ** (k - 1) + 1, TIME), min(2**k, TIME)) if k else (1, 1)


def peaks_kernel(widths_ref, series_ref, same_hbm, peaks_hbm, wide, sums, best, same_sem, sems):
    beams, samples, width = series_ref.shape
    same = pltpu.make_async_copy(series_ref, same_hbm, same_sem)
    same.start()
    for j in range(width // LANES):
        lanes = slice(j * LANES, (j + 1) * LANES)
        wide[j] = series_ref[:, :, lanes].astype(jnp.float32).reshape(beams * samples, LANES)
        total = jnp.zeros((beams, LANES), jnp.float32)
        sums[0, :, lanes] = total
        for t in range(samples):
            total = total + wide[j, pl.ds(t, beams, stride=samples), :]
            sums[t + 1, :, lanes] = total
    for t in range(samples + 1, sums.shape[0]):
        sums[t] = jnp.full((beams, width), -1e30, jnp.float32)
    copies = []
    for k in range(best.shape[0]):
        reach = widths_ref[k]
        value = sums[reach]
        for t in range(1, samples + 1 - width_range(k)[0]):
            value = jnp.maximum(value, sums[t + reach] - sums[t])
        best[k] = value / jnp.sqrt(jnp.full((beams, width), reach).astype(jnp.float32))
        copies.append(pltpu.make_async_copy(best.at[k], peaks_hbm.at[k], sems.at[k]))
        copies[-1].start()
    same.wait()
    for copy in copies:
        copy.wait()


def peaks(widths, series):
    beams, samples, width = series.shape
    count = widths.shape[0]
    rows = max(samples + 1 - low + high for low, high in map(width_range, range(count)))
    return pl.pallas_call(
        peaks_kernel,
        in_specs=[pl.BlockSpec(memory_space=pltpu.SMEM), pl.BlockSpec(memory_space=pltpu.VMEM)],
        out_specs=[pl.BlockSpec(memory_space=pltpu.HBM)] * 2,
        out_shape=[
            jax.ShapeDtypeStruct(series.shape, series.dtype),
            jax.ShapeDtypeStruct((count, beams, width), jnp.float32),
        ],
        scratch_shapes=[
            pltpu.VMEM((width // LANES, beams * samples, LANES), jnp.float32),
            pltpu.VMEM((rows, beams, width), jnp.float32),
            pltpu.VMEM((count, beams, width), jnp.float32),
            pltpu.SemaphoreType.DMA,
            pltpu.SemaphoreType.DMA((count,)),
        ],
        compiler_params=pltpu.CompilerParams(vmem_limit_bytes=8 * MIB),
        name="peaks",
    )(widths, series)


def gathered(block, axis):
    count = lax.axis_size(axis)
    position = lax.axis_index(axis)
    whole = block[None]
    step = 1
    while step < count:
        parts = [whole]
        for k in range(1, 4):
            parts.append(lax.ppermute(whole, axis, [(i, i ^ k * step) for i in range(count)]))
        for bit in (1, 2):
            odd = position & bit * step != 0
            parts = [jnp.where(odd, parts[k ^ bit], parts[k]) for k in range(4)]
        whole = jnp.concatenate(parts)
        step *= 4
    return whole


def exchanged(block, axes):
    return lax.all_to_all(block, axes, split_axis=0, concat_axis=0, tiled=True)


def shards(voltages, gains, shifts, widths):
    groups = lax.axis_size("beam")
    received = exchanged(calibrate(voltages, gains), "beam")
    matrix, shifts = lax.optimization_barrier((steering(groups), shifts))
    table = jnp.transpose(gathered(shifts, "freq"), (1, 0, 2))
    early = (matrix, table, jnp.maximum(widths, 1))
    received, matrix, table, reach = lax.optimization_barrier((received, *early))
    detected = detect(received.reshape(2 * FEEDS, received.shape[2]), matrix)
    spread = exchanged(detected.reshape(FEEDS, -1, LANES), ("freq", "beam"))
    series = exchanged(tree(spread.reshape(detected.shape), table), "freq")
    return tuple(peaks(reach, series))


def solution(mesh):
    return jax.shard_map(
        shards,
        mesh=mesh,
        in_specs=(P(None, "beam", None, "freq"), P(None, "beam", "freq"), P(None, "freq"), P()),
        out_specs=(P("beam", None, "freq"), P(None, "beam", "freq")),
        check_vma=False,
    )
```

```python
import functools
import math

import jax
import jax.numpy as jnp
from jax import lax
from jax.experimental import pallas as pl
from jax.experimental.pallas import tpu as pltpu
from jax.sharding import PartitionSpec as P

FEEDS = 256
CHAN_SUM = 4
NSUB = 4096
TIME = 16
LANES = 128
CORES = 2
PITCH = 24
MIB = 1024 * 1024


def steering(groups, chip):
    size = FEEDS // groups
    chips = groups // CORES
    span = FEEDS // chips
    row = lax.broadcasted_iota(jnp.int32, (2 * FEEDS, LANES), 0)
    col = lax.broadcasted_iota(jnp.int32, (2 * FEEDS, LANES), 1)
    out_part = row // FEEDS
    beam = row % groups * size + row % FEEDS // groups
    rest = col // (2 * size) % CORES * size + col % size
    quarters = out_part - col // size % 2
    angles = (beam * rest + quarters * (FEEDS // 4) & FEEDS - 1).astype(jnp.float32) * (2.0 * math.pi / FEEDS)
    factor = 1.0 / math.sqrt(FEEDS)
    cosine = jnp.cos(angles) * factor
    sine = jnp.sin(angles) * factor
    blocks = []
    for first in range(0, chips, LANES // (2 * span)):
        source = chip - (first + col // (2 * span)) & chips - 1
        turn = beam * source & chips - 1
        whole_cosine = eighth_cosine(turn)
        whole_sine = eighth_cosine(turn - chips // 4 & chips - 1)
        blocks.append((whole_cosine * cosine - whole_sine * sine).astype(jnp.bfloat16))
    return jnp.concatenate(blocks, axis=1)


def eighth_cosine(turn):
    size = jnp.where(turn % 2 == 1, math.sqrt(0.5), jnp.where(turn % 4 == 2, 0.0, 1.0))
    return jnp.where((turn > 2) & (turn < 6), -size, size)


def calibrate_kernel(where_ref, volt_hbm, gain_hbm, *rest, own):
    if own:
        outs, rest = rest[:1], rest[1:]
    else:
        begun_ref, outs, rest = rest[0], rest[1:9], rest[9:]
    volt, gain, wide, in_sems = rest
    chunks, _, feeds, samples, _ = volt.shape
    chip, core = where_ref[0], where_ref[1]

    def arriving(j):
        lanes = pl.ds(pl.multiple_of((core * chunks + j) * LANES, LANES), LANES)
        return (
            pltpu.make_async_copy(volt_hbm.at[:, :, :, lanes], volt.at[j], in_sems.at[0, j]),
            pltpu.make_async_copy(gain_hbm.at[:, :, lanes], gain.at[j], in_sems.at[1, j]),
        )

    for j in range(chunks):
        for copy in arriving(j):
            copy.start()
    if not own:
        for k, out in enumerate(outs):
            for t in range(2):
                out[t, core] = begun_ref[2 * (chip + k & len(outs) - 1) + t]
    for j in range(chunks):
        lanes = slice(j * LANES, (j + 1) * LANES)
        for copy in arriving(j):
            copy.wait()
        for part in range(2):
            block = volt[j, part].astype(jnp.float32)
            for f in range(feeds):
                wide[j, part, f * PITCH : f * PITCH + samples] = block[f]
        gain_re = gain[j, 0]
        gain_im = gain[j, 1]
        for k in range(samples // 2):
            for t in range(2):
                sample = 2 * k + t if own else 2 * (chip + k & samples // 2 - 1) + t
                volt_re = wide[j, 0, pl.ds(sample, feeds, stride=PITCH), :]
                volt_im = wide[j, 1, pl.ds(sample, feeds, stride=PITCH), :]
                real = (gain_re * volt_re - gain_im * volt_im).astype(jnp.bfloat16)
                imag = (gain_re * volt_im + gain_im * volt_re).astype(jnp.bfloat16)
                if own:
                    outs[0][sample, :feeds, lanes] = real
                    outs[0][sample, feeds:, lanes] = imag
                else:
                    outs[k][t, 1 - core, :feeds, lanes] = real
                    outs[k][t, 1 - core, feeds:, lanes] = imag


def calibrate(where, voltages, gains, begun=None):
    _, feeds, samples, width = voltages.shape
    chunks = width // CORES // LANES
    own = begun is None
    shape = (samples, 2 * feeds, width // CORES)
    if own:
        out_shape = jax.ShapeDtypeStruct(shape, jnp.bfloat16)
    else:
        out_shape = [jax.ShapeDtypeStruct((2, CORES) + shape[1:], jnp.bfloat16)] * (samples // 2)
    operands = (where, voltages, gains) + (() if own else (begun,))
    return pl.pallas_call(
        functools.partial(calibrate_kernel, own=own),
        in_specs=[pl.BlockSpec(memory_space=pltpu.SMEM)]
        + [pl.BlockSpec(memory_space=pl.ANY)] * 2
        + [pl.BlockSpec(memory_space=pltpu.VMEM)] * (not own),
        out_shape=out_shape,
        scratch_shapes=[
            pltpu.VMEM((chunks, 2, feeds, samples, LANES), jnp.bfloat16),
            pltpu.VMEM((chunks, 2, feeds, LANES), jnp.float32),
            pltpu.VMEM((chunks, 2, feeds * PITCH, LANES), jnp.float32),
            pltpu.SemaphoreType.DMA((2, chunks)),
        ],
        compiler_params=pltpu.CompilerParams(vmem_limit_bytes=(58 if own else 16) * MIB),
        name="calibrate",
    )(*operands)


def detect_kernel(matrix_ref, *rest):
    parts, (out_ref, scratch) = rest[:-2], rest[-2:]
    pair, _, _, width = parts[0].shape
    step = 256
    channel = lax.broadcasted_iota(jnp.int32, (step, width // CHAN_SUM), 0)
    group = lax.broadcasted_iota(jnp.int32, (step, width // CHAN_SUM), 1)
    for t in range(pair):
        total = jnp.zeros((FEEDS, width // CHAN_SUM), jnp.float32)
        for j in range(width // step):
            cols = slice(j * step, (j + 1) * step)
            x = jnp.concatenate([part[t, core, :, cols] for part in parts for core in range(CORES)], axis=0)
            formed = jnp.dot(matrix_ref[...], x, preferred_element_type=jnp.float32)
            power = formed[:FEEDS] * formed[:FEEDS] + formed[FEEDS:] * formed[FEEDS:]
            sums = []
            for lane in range(0, step, LANES):
                part = power[:, lane : lane + LANES]
                part = part + pltpu.roll(part, LANES - 1, 1)
                sums.append(part + pltpu.roll(part, LANES - 2, 1))
            picking = (channel + j * step == group * CHAN_SUM).astype(jnp.bfloat16)
            summed = jnp.concatenate(sums, axis=1).astype(jnp.bfloat16)
            total += jnp.dot(summed, picking, preferred_element_type=jnp.float32)
        scratch[pl.ds(t, FEEDS, stride=pair), :] = total
    out_ref[...] = scratch[...].astype(jnp.bfloat16)


def detect(parts, matrix):
    shape = (FEEDS * parts[0].shape[0], parts[0].shape[3] // CHAN_SUM)
    return pl.pallas_call(
        detect_kernel,
        out_shape=jax.ShapeDtypeStruct(shape, jnp.bfloat16),
        scratch_shapes=[pltpu.VMEM(shape, jnp.float32)],
        compiler_params=pltpu.CompilerParams(vmem_limit_bytes=16 * MIB),
        name="detect",
    )(matrix, *parts)


def shifted(rows, bits):
    zero = jnp.zeros_like(rows[0])
    count = len(rows)
    for position, chosen in enumerate(bits):
        step = 1 << position
        rows = [jnp.where(chosen, rows[t + step] if t + step < count else zero, rows[t]) for t in range(count)]
    return rows


def digits(offsets, most):
    return [(offsets >> position & 1) == 1 for position in range(most.bit_length())]


def merged(lower_rows, higher_rows, bits):
    return [x + y for x, y in zip(lower_rows, shifted(higher_rows, bits))]


def folded(rows, axis, half, bits):
    place = lax.broadcasted_iota(jnp.int32, rows[0].shape, axis)
    upper = (place & half) != 0
    facing = [jnp.take_along_axis(x, place ^ half, axis=axis) for x in rows]
    lower_rows = [jnp.where(upper, y, x) for x, y in zip(rows, facing)]
    higher_rows = [jnp.where(upper, x, y) for x, y in zip(rows, facing)]
    return merged(lower_rows, higher_rows, bits)


def tree_kernel(detected_ref, shifts_ref, out_ref, wide, held, turned):
    blocks, samples, width = out_ref.shape
    pieces = width // LANES
    scale = 1.0 / (8.0 * math.sqrt(NSUB))
    wide[...] = detected_ref[...].astype(jnp.float32)

    def bits_of(section, group, piece):
        offsets = shifts_ref[section, group * 8 : (group + 1) * 8, piece * LANES : (piece + 1) * LANES]
        return digits(offsets, min(1 << section, 8))

    lane_bits = LANES.bit_length() - 1
    for group in range(blocks // 8):
        for piece in range(pieces):
            rows = []
            for t in range(samples):
                first = (group * 8 * samples + t // 2 * 2 + piece) * pieces + t % 2
                rows.append(wide[pl.ds(first, 8, stride=samples * pieces), :])
            mean = functools.reduce(jnp.add, rows) * (1.0 / samples)
            rows = [row - mean for row in rows]
            for section in range(lane_bits):
                rows = folded(rows, 1, 1 << section, bits_of(section, group, piece))
            for t in range(samples):
                held[piece, group, t] = rows[t]
    for group in range(blocks // 8):
        for piece in range(pieces):
            lower_rows = [held[0, group, t] for t in range(samples)]
            higher_rows = [held[1, group, t] for t in range(samples)]
            rows = merged(lower_rows, higher_rows, bits_of(lane_bits, group, piece))
            for bit in range(3):
                section = lane_bits + 1 + bit
                rows = folded(rows, 0, 1 << bit, bits_of(section, group, piece))
            for t in range(samples):
                first = (group * pieces + piece) * samples * 8 + t * 8
                wide[first : first + 8, :] = rows[t]
    for piece in range(pieces):
        parts = []
        for group in range(2):
            first = (group * pieces + piece) * samples * 8
            parts.append([wide[first + t * 8 : first + t * 8 + 8, :] for t in range(samples)])
        for group in range(2):
            rows = merged(parts[0], parts[1], bits_of(lane_bits + 4, group, piece))
            for t in range(samples):
                turned[piece, pl.ds(group * 8 * samples + t, 8, stride=samples), :] = rows[t] * scale
        block = turned[piece].reshape(blocks, samples, LANES)
        out_ref[:, :, piece * LANES : (piece + 1) * LANES] = block.astype(jnp.bfloat16)


def tree(detected, shifts):
    sections, blocks, width = shifts.shape
    pieces = width // LANES
    rows = detected.shape[0]
    return pl.pallas_call(
        tree_kernel,
        out_shape=jax.ShapeDtypeStruct((blocks, TIME, width), jnp.bfloat16),
        scratch_shapes=[
            pltpu.VMEM((rows, LANES), jnp.float32),
            pltpu.VMEM((pieces, blocks // 8, TIME, 8, LANES), jnp.float32),
            pltpu.VMEM((pieces, blocks * TIME, LANES), jnp.float32),
        ],
        compiler_params=pltpu.CompilerParams(vmem_limit_bytes=8 * MIB),
        name="tree",
    )(detected, shifts)


def width_range(k):
    return (min(2 ** (k - 1) + 1, TIME), min(2**k, TIME)) if k else (1, 1)


def peaks_kernel(widths_ref, series_ref, same_hbm, peaks_hbm, wide, sums, best, same_sem, sems):
    beams, samples, width = series_ref.shape
    same = pltpu.make_async_copy(series_ref, same_hbm, same_sem)
    same.start()
    for j in range(width // LANES):
        lanes = slice(j * LANES, (j + 1) * LANES)
        wide[j] = series_ref[:, :, lanes].astype(jnp.float32).reshape(beams * samples, LANES)
        total = jnp.zeros((beams, LANES), jnp.float32)
        sums[0, :, lanes] = total
        for t in range(samples):
            total = total + wide[j, pl.ds(t, beams, stride=samples), :]
            sums[t + 1, :, lanes] = total
    for t in range(samples + 1, sums.shape[0]):
        sums[t] = jnp.full((beams, width), -1e30, jnp.float32)
    copies = []
    for k in range(best.shape[0]):
        reach = widths_ref[k]
        value = sums[reach]
        for t in range(1, samples + 1 - width_range(k)[0]):
            value = jnp.maximum(value, sums[t + reach] - sums[t])
        best[k] = value / jnp.sqrt(jnp.full((beams, width), reach).astype(jnp.float32))
        copies.append(pltpu.make_async_copy(best.at[k], peaks_hbm.at[k], sems.at[k]))
        copies[-1].start()
    same.wait()
    for copy in copies:
        copy.wait()


def peaks(widths, series):
    beams, samples, width = series.shape
    count = widths.shape[0]
    rows = max(samples + 1 - low + high for low, high in map(width_range, range(count)))
    return pl.pallas_call(
        peaks_kernel,
        in_specs=[pl.BlockSpec(memory_space=pltpu.SMEM), pl.BlockSpec(memory_space=pltpu.VMEM)],
        out_specs=[pl.BlockSpec(memory_space=pltpu.HBM)] * 2,
        out_shape=[
            jax.ShapeDtypeStruct(series.shape, series.dtype),
            jax.ShapeDtypeStruct((count, beams, width), jnp.float32),
        ],
        scratch_shapes=[
            pltpu.VMEM((width // LANES, beams * samples, LANES), jnp.float32),
            pltpu.VMEM((rows, beams, width), jnp.float32),
            pltpu.VMEM((count, beams, width), jnp.float32),
            pltpu.SemaphoreType.DMA,
            pltpu.SemaphoreType.DMA((count,)),
        ],
        compiler_params=pltpu.CompilerParams(vmem_limit_bytes=8 * MIB),
        name="peaks",
    )(widths, series)


def exchanged(block, axes):
    return lax.all_to_all(block, axes, split_axis=0, concat_axis=0, tiled=True)


def travelled(messages):
    groups = lax.axis_size("beam")
    chips = len(messages)

    def sent(block, distance):
        return lax.ppermute(block, "beam", [(i, (i + distance * CORES) % groups) for i in range(groups)])

    got = list(messages)
    for k in [2, chips - 2] + list(range(3, chips - 2)):
        got[k] = sent(messages[k], k)
    near = lax.optimization_barrier((messages[1], messages[-1], got[2], got[-2]))
    got[1], got[-1], got[2], got[-2] = sent(near[0], 1), sent(near[1], chips - 1), near[2], near[3]
    return got


def shards(voltages, gains, shifts, widths):
    groups = lax.axis_size("beam")
    place = lax.axis_index("beam").astype(jnp.int32)
    chip, core = place >> 1, place & 1
    where = jnp.stack([chip, core])
    padded = jnp.concatenate([shifts, jnp.zeros((64 - shifts.shape[0], shifts.shape[1]), jnp.int32)])
    table = lax.all_gather(padded, "freq")[:, : shifts.shape[0]]
    swap = [(i, i ^ 1) for i in range(groups)]
    other = [lax.ppermute(block, "beam", swap) for block in (voltages, gains)]
    messages = calibrate(where, *other, calibrate(where, voltages, gains))
    received = travelled(messages)
    early = (steering(groups, chip), jnp.maximum(widths, 1))
    received, matrix, reach = lax.optimization_barrier((received, *early))
    detected = detect(received, matrix)
    spread = exchanged(detected.reshape(FEEDS, -1, LANES), ("freq", "beam"))
    series = exchanged(tree(spread.reshape(detected.shape), jnp.transpose(table, (1, 0, 2))), "freq")
    return tuple(peaks(reach, series))


def solution(mesh):
    return jax.shard_map(
        shards,
        mesh=mesh,
        in_specs=(P(None, "beam", None, "freq"), P(None, "beam", "freq"), P(None, "freq"), P()),
        out_specs=(P("beam", None, "freq"), P(None, "beam", "freq")),
        check_vma=False,
    )
```

```python
import functools
import math

import jax
import jax.numpy as jnp
from jax import lax
from jax.experimental import pallas as pl
from jax.experimental.pallas import tpu as pltpu
from jax.sharding import PartitionSpec as P

FEEDS = 256
CHAN_SUM = 4
NSUB = 4096
TIME = 16
LANES = 128
CORES = 2
PITCH = 24
MIB = 1024 * 1024


def steering(groups, chip):
    size = FEEDS // groups
    chips = groups // CORES
    span = FEEDS // chips
    row = lax.broadcasted_iota(jnp.int32, (2 * FEEDS, LANES), 0)
    col = lax.broadcasted_iota(jnp.int32, (2 * FEEDS, LANES), 1)
    out_part = row // FEEDS
    beam = row % groups * size + row % FEEDS // groups
    rest = col // (2 * size) % CORES * size + col % size
    quarters = out_part - col // size % 2
    phase = beam * rest + quarters * (FEEDS // 4) + chip * FEEDS & FEEDS - 1
    angles = phase.astype(jnp.float32) * (2.0 * math.pi / FEEDS)
    factor = 1.0 / math.sqrt(FEEDS)
    cosine, sine = lax.optimization_barrier((jnp.cos(angles) * factor, jnp.sin(angles) * factor))
    blocks = []
    for first in range(0, chips, LANES // (2 * span)):
        source = chip - (first + col // (2 * span)) & chips - 1
        turn = beam * source & chips - 1
        whole_cosine = eighth_cosine(turn)
        whole_sine = eighth_cosine(turn - chips // 4 & chips - 1)
        blocks.append((whole_cosine * cosine - whole_sine * sine).astype(jnp.bfloat16))
    return jnp.concatenate(blocks, axis=1)


def eighth_cosine(turn):
    size = jnp.where(turn % 2 == 1, math.sqrt(0.5), jnp.where(turn % 4 == 2, 0.0, 1.0))
    return jnp.where((turn > 2) & (turn < 6), -size, size)


def calibrate_kernel(where_ref, volt_hbm, gain_hbm, *rest, own):
    volt, gain, wide, in_sems, sems = rest[-5:]
    chunks, _, feeds, samples, _ = volt.shape
    chip, core = where_ref[0], where_ref[1]
    if own:
        out_hbm, done = rest[:2]
    else:
        begun_hbm, outs = rest[0], rest[1 : 1 + samples // 2]

    def arriving(j):
        lanes = pl.ds(pl.multiple_of((core * chunks + j) * LANES, LANES), LANES)
        return (
            pltpu.make_async_copy(volt_hbm.at[:, :, :, lanes], volt.at[j], in_sems.at[0, j]),
            pltpu.make_async_copy(gain_hbm.at[:, :, lanes], gain.at[j], in_sems.at[1, j]),
        )

    def leaving(j):
        return pltpu.make_async_copy(done.at[j], out_hbm.at[:, :, pl.ds(j * LANES, LANES)], sems.at[j])

    def joining(k):
        pair = begun_hbm.at[pl.ds(2 * (chip + k & samples // 2 - 1), 2)]
        return pltpu.make_async_copy(pair, outs[k].at[:, core], sems.at[k])

    for j in range(chunks):
        for copy in arriving(j):
            copy.start()
    if not own:
        for k in range(len(outs)):
            joining(k).start()
    for j in range(chunks):
        lanes = slice(j * LANES, (j + 1) * LANES)
        for copy in arriving(j):
            copy.wait()
        for part in range(2):
            block = volt[j, part].astype(jnp.float32)
            for f in range(feeds):
                wide[j, part, f * PITCH : f * PITCH + samples] = block[f]
        gain_re = gain[j, 0]
        gain_im = gain[j, 1]
        for k in range(samples // 2):
            for t in range(2):
                sample = 2 * k + t if own else 2 * (chip + k & samples // 2 - 1) + t
                volt_re = wide[j, 0, pl.ds(sample, feeds, stride=PITCH), :]
                volt_im = wide[j, 1, pl.ds(sample, feeds, stride=PITCH), :]
                real = (gain_re * volt_re - gain_im * volt_im).astype(jnp.bfloat16)
                imag = (gain_re * volt_im + gain_im * volt_re).astype(jnp.bfloat16)
                if own:
                    done[j, sample, :feeds] = real
                    done[j, sample, feeds:] = imag
                else:
                    outs[k][t, 1 - core, :feeds, lanes] = real
                    outs[k][t, 1 - core, feeds:, lanes] = imag
        if own:
            leaving(j).start()
    if own:
        for j in range(chunks):
            leaving(j).wait()
    else:
        for k in range(len(outs)):
            joining(k).wait()


def calibrate(where, voltages, gains, begun=None):
    _, feeds, samples, width = voltages.shape
    chunks = width // CORES // LANES
    own = begun is None
    shape = (samples, 2 * feeds, width // CORES)
    if own:
        out_shape = jax.ShapeDtypeStruct(shape, jnp.bfloat16)
        out_specs = pl.BlockSpec(memory_space=pltpu.HBM)
    else:
        out_shape = [jax.ShapeDtypeStruct((2, CORES) + shape[1:], jnp.bfloat16)] * (samples // 2)
        out_specs = [pl.BlockSpec(memory_space=pltpu.VMEM)] * (samples // 2)
    operands = (where, voltages, gains) + (() if own else (begun,))
    return pl.pallas_call(
        functools.partial(calibrate_kernel, own=own),
        in_specs=[pl.BlockSpec(memory_space=pltpu.SMEM)] + [pl.BlockSpec(memory_space=pl.ANY)] * (len(operands) - 1),
        out_specs=out_specs,
        out_shape=out_shape,
        scratch_shapes=[pltpu.VMEM((chunks, samples, 2 * feeds, LANES), jnp.bfloat16)] * own
        + [
            pltpu.VMEM((chunks, 2, feeds, samples, LANES), jnp.bfloat16),
            pltpu.VMEM((chunks, 2, feeds, LANES), jnp.float32),
            pltpu.VMEM((chunks, 2, feeds * PITCH, LANES), jnp.float32),
            pltpu.SemaphoreType.DMA((2, chunks)),
            pltpu.SemaphoreType.DMA((chunks if own else samples // 2,)),
        ],
        compiler_params=pltpu.CompilerParams(vmem_limit_bytes=(58 if own else 8) * MIB),
        name="calibrate",
    )(*operands)


def detect_kernel(matrix_ref, *rest):
    parts, (out_ref, scratch) = rest[:-2], rest[-2:]
    pair, _, _, width = parts[0].shape
    step = 256
    groups = width // CHAN_SUM
    channel = lax.broadcasted_iota(jnp.int32, (width, groups), 0)
    picking = channel == lax.broadcasted_iota(jnp.int32, (width, groups), 1) * CHAN_SUM
    picking = picking.astype(jnp.bfloat16)
    for t in range(pair):
        sums = []
        for first in range(0, width, step):
            cols = slice(first, first + step)
            x = jnp.concatenate([part[t, core, :, cols] for part in parts for core in range(CORES)], axis=0)
            formed = jnp.dot(matrix_ref[...], x, preferred_element_type=jnp.float32)
            power = formed[:FEEDS] * formed[:FEEDS] + formed[FEEDS:] * formed[FEEDS:]
            for lane in range(0, step, LANES):
                part = power[:, lane : lane + LANES]
                part = part + pltpu.roll(part, LANES - 1, 1)
                sums.append((part + pltpu.roll(part, LANES - 2, 1)).astype(jnp.bfloat16))
        summed = jnp.concatenate(sums, axis=1)
        scratch[pl.ds(t, FEEDS, stride=pair), :] = jnp.dot(summed, picking, preferred_element_type=jnp.float32)
    out_ref[...] = scratch[...].astype(jnp.bfloat16)


def detect(parts, matrix):
    shape = (FEEDS * parts[0].shape[0], parts[0].shape[3] // CHAN_SUM)
    return pl.pallas_call(
        detect_kernel,
        out_shape=jax.ShapeDtypeStruct(shape, jnp.bfloat16),
        scratch_shapes=[pltpu.VMEM(shape, jnp.float32)],
        compiler_params=pltpu.CompilerParams(vmem_limit_bytes=16 * MIB),
        name="detect",
    )(matrix, *parts)


def shifted(rows, bits):
    zero = jnp.zeros_like(rows[0])
    count = len(rows)
    for position, chosen in enumerate(bits):
        step = 1 << position
        rows = [jnp.where(chosen, rows[t + step] if t + step < count else zero, rows[t]) for t in range(count)]
    return rows


def digits(offsets, most):
    return [(offsets >> position & 1) == 1 for position in range(most.bit_length())]


def merged(lower_rows, higher_rows, bits):
    return [x + y for x, y in zip(lower_rows, shifted(higher_rows, bits))]


def folded(rows, axis, half, bits):
    place = lax.broadcasted_iota(jnp.int32, rows[0].shape, axis)
    upper = (place & half) != 0
    facing = [jnp.take_along_axis(x, place ^ half, axis=axis) for x in rows]
    lower_rows = [jnp.where(upper, y, x) for x, y in zip(rows, facing)]
    higher_rows = [jnp.where(upper, x, y) for x, y in zip(rows, facing)]
    return merged(lower_rows, higher_rows, bits)


def tree_kernel(detected_ref, shifts_ref, out_ref, wide, held, turned):
    blocks, samples, width = out_ref.shape
    pieces = width // LANES
    scale = 1.0 / (8.0 * math.sqrt(NSUB))
    length = samples * pieces
    pitch = length + 8
    for q in range(blocks):
        wide[q * pitch : q * pitch + length] = detected_ref[q * length : (q + 1) * length].astype(jnp.float32)

    def bits_of(section, group, piece):
        offsets = shifts_ref[section, group * 8 : (group + 1) * 8, piece * LANES : (piece + 1) * LANES]
        return digits(offsets, min(1 << section, 8))

    lane_bits = LANES.bit_length() - 1
    for group in range(blocks // 8):
        for piece in range(pieces):
            rows = []
            for t in range(samples):
                first = group * 8 * pitch + t // 2 * 4 + piece * 2 + t % 2
                rows.append(wide[pl.ds(first, 8, stride=pitch), :])
            mean = functools.reduce(jnp.add, rows) * (1.0 / samples)
            rows = [row - mean for row in rows]
            for section in range(lane_bits):
                rows = folded(rows, 1, 1 << section, bits_of(section, group, piece))
            for t in range(samples):
                held[piece, group, t] = rows[t]
    for group in range(blocks // 8):
        for piece in range(pieces):
            lower_rows = [held[0, group, t] for t in range(samples)]
            higher_rows = [held[1, group, t] for t in range(samples)]
            rows = merged(lower_rows, higher_rows, bits_of(lane_bits, group, piece))
            for bit in range(3):
                section = lane_bits + 1 + bit
                rows = folded(rows, 0, 1 << bit, bits_of(section, group, piece))
            for t in range(samples):
                first = (group * pieces + piece) * samples * 8 + t * 8
                wide[first : first + 8, :] = rows[t]
    for piece in range(pieces):
        parts = []
        for group in range(2):
            first = (group * pieces + piece) * samples * 8
            parts.append([wide[first + t * 8 : first + t * 8 + 8, :] for t in range(samples)])
        for group in range(2):
            rows = merged(parts[0], parts[1], bits_of(lane_bits + 4, group, piece))
            for t in range(samples):
                turned[piece, pl.ds(group * 8 * PITCH + t, 8, stride=PITCH), :] = rows[t] * scale
        for q in range(blocks):
            block = turned[piece, q * PITCH : q * PITCH + samples, :]
            out_ref[q, :, piece * LANES : (piece + 1) * LANES] = block.astype(jnp.bfloat16)


def tree(detected, shifts):
    sections, blocks, width = shifts.shape
    pieces = width // LANES
    rows = detected.shape[0]
    return pl.pallas_call(
        tree_kernel,
        out_shape=jax.ShapeDtypeStruct((blocks, TIME, width), jnp.bfloat16),
        scratch_shapes=[
            pltpu.VMEM((rows + 8 * blocks, LANES), jnp.float32),
            pltpu.VMEM((pieces, blocks // 8, TIME, 8, LANES), jnp.float32),
            pltpu.VMEM((pieces, blocks * PITCH, LANES), jnp.float32),
        ],
        compiler_params=pltpu.CompilerParams(vmem_limit_bytes=8 * MIB),
        name="tree",
    )(detected, shifts)


def width_range(k):
    return (min(2 ** (k - 1) + 1, TIME), min(2**k, TIME)) if k else (1, 1)


def peaks_kernel(widths_ref, series_ref, same_hbm, peaks_hbm, wide, sums, best, same_sem, sems):
    beams, samples, width = series_ref.shape
    same = pltpu.make_async_copy(series_ref, same_hbm, same_sem)
    same.start()
    for j in range(width // LANES):
        lanes = slice(j * LANES, (j + 1) * LANES)
        wide[j] = series_ref[:, :, lanes].astype(jnp.float32).reshape(beams * samples, LANES)
        total = jnp.zeros((beams, LANES), jnp.float32)
        sums[0, :, lanes] = total
        for t in range(samples):
            total = total + wide[j, pl.ds(t, beams, stride=samples), :]
            sums[t + 1, :, lanes] = total
    for t in range(samples + 1, sums.shape[0]):
        sums[t] = jnp.full((beams, width), -1e30, jnp.float32)
    copies = []
    for k in range(best.shape[0]):
        reach = widths_ref[k]
        value = sums[reach]
        for t in range(1, samples + 1 - width_range(k)[0]):
            value = jnp.maximum(value, sums[t + reach] - sums[t])
        best[k] = value / jnp.sqrt(jnp.full((beams, width), reach).astype(jnp.float32))
        copies.append(pltpu.make_async_copy(best.at[k], peaks_hbm.at[k], sems.at[k]))
        copies[-1].start()
    same.wait()
    for copy in copies:
        copy.wait()


def peaks(widths, series):
    beams, samples, width = series.shape
    count = widths.shape[0]
    rows = max(samples + 1 - low + high for low, high in map(width_range, range(count)))
    return pl.pallas_call(
        peaks_kernel,
        in_specs=[pl.BlockSpec(memory_space=pltpu.SMEM), pl.BlockSpec(memory_space=pltpu.VMEM)],
        out_specs=[pl.BlockSpec(memory_space=pltpu.HBM)] * 2,
        out_shape=[
            jax.ShapeDtypeStruct(series.shape, series.dtype),
            jax.ShapeDtypeStruct((count, beams, width), jnp.float32),
        ],
        scratch_shapes=[
            pltpu.VMEM((width // LANES, beams * samples, LANES), jnp.float32),
            pltpu.VMEM((rows, beams, width), jnp.float32),
            pltpu.VMEM((count, beams, width), jnp.float32),
            pltpu.SemaphoreType.DMA,
            pltpu.SemaphoreType.DMA((count,)),
        ],
        compiler_params=pltpu.CompilerParams(vmem_limit_bytes=8 * MIB),
        name="peaks",
    )(widths, series)


def exchanged(block, axes):
    return lax.all_to_all(block, axes, split_axis=0, concat_axis=0, tiled=True)


def shards(voltages, gains, shifts, widths):
    groups = lax.axis_size("beam")
    place = lax.axis_index("beam").astype(jnp.int32)
    chip, core = place >> 1, place & 1
    where = jnp.stack([chip, core])
    swap = [(i, i ^ 1) for i in range(groups)]
    other = [lax.ppermute(block, "beam", swap) for block in (voltages, gains)]
    messages = calibrate(where, *other, calibrate(where, voltages, gains))

    def sent(block, distance):
        return lax.ppermute(block, "beam", [(i, (i + distance * CORES) % groups) for i in range(groups)])

    got = list(messages)
    for k in (2, 6, 3, 4, 5):
        got[k] = sent(messages[k], k)
    late = (messages[1], messages[7], got[2], got[6], chip, shifts)
    near, far, got[2], got[6], chip, shifts = lax.optimization_barrier(late)
    got[1], got[7] = sent(near, 1), sent(far, 7)
    short = jnp.concatenate([shifts.astype(jnp.bfloat16), jnp.zeros((16 - shifts.shape[0], shifts.shape[1]), jnp.bfloat16)])
    table = exchanged(jnp.broadcast_to(short[None], (lax.axis_size("freq"),) + short.shape), "freq")
    table = jnp.transpose(table[:, : shifts.shape[0]].astype(jnp.int32), (1, 0, 2))
    early = (steering(groups, chip), jnp.maximum(widths, 1), table)
    received, matrix, reach, table = lax.optimization_barrier((got, *early))
    detected = detect(received, matrix)
    spread = exchanged(detected.reshape(FEEDS, -1, LANES), ("freq", "beam"))
    series = exchanged(tree(spread.reshape(detected.shape), table), "freq")
    return tuple(peaks(reach, series))


def solution(mesh):
    return jax.shard_map(
        shards,
        mesh=mesh,
        in_specs=(P(None, "beam", None, "freq"), P(None, "beam", "freq"), P(None, "freq"), P()),
        out_specs=(P("beam", None, "freq"), P(None, "beam", "freq")),
        check_vma=False,
    )
```

```python
import functools
import math

import jax
import jax.numpy as jnp
from jax import lax
from jax.experimental import pallas as pl
from jax.experimental.pallas import tpu as pltpu
from jax.sharding import PartitionSpec as P

FEEDS = 256
CHAN_SUM = 4
NSUB = 4096
TIME = 16
LANES = 128
CORES = 2
PITCH = 24
MIB = 1024 * 1024


def steering(groups, chip):
    size = FEEDS // groups
    chips = groups // CORES
    span = FEEDS // chips
    row = lax.broadcasted_iota(jnp.int32, (2 * FEEDS, LANES), 0)
    col = lax.broadcasted_iota(jnp.int32, (2 * FEEDS, LANES), 1)
    out_part = row // FEEDS
    beam = row % groups * size + row % FEEDS // groups
    rest = col // (2 * size) % CORES * size + col % size
    quarters = out_part - col // size % 2
    phase = beam * rest + quarters * (FEEDS // 4) + chip * FEEDS & FEEDS - 1
    angles = phase.astype(jnp.float32) * (2.0 * math.pi / FEEDS)
    factor = 1.0 / math.sqrt(FEEDS)
    cosine, sine = lax.optimization_barrier((jnp.cos(angles) * factor, jnp.sin(angles) * factor))
    blocks = []
    for first in range(0, chips, LANES // (2 * span)):
        source = chip - (first + col // (2 * span)) & chips - 1
        turn = beam * source & chips - 1
        whole_cosine = eighth_cosine(turn)
        whole_sine = eighth_cosine(turn - chips // 4 & chips - 1)
        blocks.append((whole_cosine * cosine - whole_sine * sine).astype(jnp.bfloat16))
    return jnp.concatenate(blocks, axis=1)


def eighth_cosine(turn):
    size = jnp.where(turn % 2 == 1, math.sqrt(0.5), jnp.where(turn % 4 == 2, 0.0, 1.0))
    return jnp.where((turn > 2) & (turn < 6), -size, size)


def calibrate_kernel(chip_ref, core_ref, volt_hbm, gain_hbm, *rest, own):
    volt, gain, wide, in_sems, sems = rest[-5:]
    chunks, _, feeds, samples, _ = volt.shape
    chip, core = chip_ref[0], core_ref[0]
    if own:
        out_hbm, done = rest[:2]
    else:
        begun_hbm, outs = rest[0], rest[1 : 1 + samples // 2]

    def arriving(j):
        lanes = pl.ds(pl.multiple_of((core * chunks + j) * LANES, LANES), LANES)
        return (
            pltpu.make_async_copy(volt_hbm.at[:, :, :, lanes], volt.at[j], in_sems.at[0, j]),
            pltpu.make_async_copy(gain_hbm.at[:, :, lanes], gain.at[j], in_sems.at[1, j]),
        )

    def leaving(j):
        return pltpu.make_async_copy(done.at[j], out_hbm.at[:, :, pl.ds(j * LANES, LANES)], sems.at[j])

    def joining(k):
        pair = begun_hbm.at[pl.ds(2 * (chip + k & samples // 2 - 1), 2)]
        return pltpu.make_async_copy(pair, outs[k].at[:, core], sems.at[k])

    for j in range(chunks):
        for copy in arriving(j):
            copy.start()
    if not own:
        for k in range(len(outs)):
            joining(k).start()
    for j in range(chunks):
        lanes = slice(j * LANES, (j + 1) * LANES)
        for copy in arriving(j):
            copy.wait()
        for part in range(2):
            block = volt[j, part].astype(jnp.float32)
            for f in range(feeds):
                wide[j, part, f * PITCH : f * PITCH + samples] = block[f]
        gain_re = gain[j, 0]
        gain_im = gain[j, 1]
        for k in range(samples // 2):
            for t in range(2):
                sample = 2 * k + t if own else 2 * (chip + k & samples // 2 - 1) + t
                volt_re = wide[j, 0, pl.ds(sample, feeds, stride=PITCH), :]
                volt_im = wide[j, 1, pl.ds(sample, feeds, stride=PITCH), :]
                real = (gain_re * volt_re - gain_im * volt_im).astype(jnp.bfloat16)
                imag = (gain_re * volt_im + gain_im * volt_re).astype(jnp.bfloat16)
                if own:
                    done[j, sample, :feeds] = real
                    done[j, sample, feeds:] = imag
                else:
                    outs[k][t, 1 - core, :feeds, lanes] = real
                    outs[k][t, 1 - core, feeds:, lanes] = imag
        if own:
            leaving(j).start()
    if own:
        for j in range(chunks):
            leaving(j).wait()
    else:
        for k in range(len(outs)):
            joining(k).wait()


def calibrate(chip, core, voltages, gains, begun=None):
    _, feeds, samples, width = voltages.shape
    chunks = width // CORES // LANES
    own = begun is None
    shape = (samples, 2 * feeds, width // CORES)
    if own:
        out_shape = jax.ShapeDtypeStruct(shape, jnp.bfloat16)
        out_specs = pl.BlockSpec(memory_space=pltpu.HBM)
    else:
        out_shape = [jax.ShapeDtypeStruct((2, CORES) + shape[1:], jnp.bfloat16)] * (samples // 2)
        out_specs = [pl.BlockSpec(memory_space=pltpu.VMEM)] * (samples // 2)
    operands = (chip.reshape(1), core.reshape(1), voltages, gains) + (() if own else (begun,))
    return pl.pallas_call(
        functools.partial(calibrate_kernel, own=own),
        in_specs=[pl.BlockSpec(memory_space=pltpu.SMEM)] * 2 + [pl.BlockSpec(memory_space=pl.ANY)] * (len(operands) - 2),
        out_specs=out_specs,
        out_shape=out_shape,
        scratch_shapes=[pltpu.VMEM((chunks, samples, 2 * feeds, LANES), jnp.bfloat16)] * own
        + [
            pltpu.VMEM((chunks, 2, feeds, samples, LANES), jnp.bfloat16),
            pltpu.VMEM((chunks, 2, feeds, LANES), jnp.float32),
            pltpu.VMEM((chunks, 2, feeds * PITCH, LANES), jnp.float32),
            pltpu.SemaphoreType.DMA((2, chunks)),
            pltpu.SemaphoreType.DMA((chunks if own else samples // 2,)),
        ],
        compiler_params=pltpu.CompilerParams(vmem_limit_bytes=(58 if own else 8) * MIB),
        name="calibrate",
    )(*operands)


def detect_kernel(matrix_ref, *rest):
    parts, (out_ref, scratch) = rest[:-2], rest[-2:]
    pair, _, _, width = parts[0].shape
    step = 256
    groups = width // CHAN_SUM
    channel = lax.broadcasted_iota(jnp.int32, (width, groups), 0)
    picking = channel == lax.broadcasted_iota(jnp.int32, (width, groups), 1) * CHAN_SUM
    picking = picking.astype(jnp.bfloat16)
    for t in range(pair):
        sums = []
        for first in range(0, width, step):
            cols = slice(first, first + step)
            x = jnp.concatenate([part[t, core, :, cols] for part in parts for core in range(CORES)], axis=0)
            formed = jnp.dot(matrix_ref[...], x, preferred_element_type=jnp.float32)
            power = formed[:FEEDS] * formed[:FEEDS] + formed[FEEDS:] * formed[FEEDS:]
            for lane in range(0, step, LANES):
                part = power[:, lane : lane + LANES]
                part = part + pltpu.roll(part, LANES - 1, 1)
                sums.append((part + pltpu.roll(part, LANES - 2, 1)).astype(jnp.bfloat16))
        summed = jnp.concatenate(sums, axis=1)
        scratch[pl.ds(t, FEEDS, stride=pair), :] = jnp.dot(summed, picking, preferred_element_type=jnp.float32)
    out_ref[...] = scratch[...].astype(jnp.bfloat16)


def detect(parts, matrix):
    shape = (FEEDS * parts[0].shape[0], parts[0].shape[3] // CHAN_SUM)
    return pl.pallas_call(
        detect_kernel,
        out_shape=jax.ShapeDtypeStruct(shape, jnp.bfloat16),
        scratch_shapes=[pltpu.VMEM(shape, jnp.float32)],
        compiler_params=pltpu.CompilerParams(vmem_limit_bytes=16 * MIB),
        name="detect",
    )(matrix, *parts)


def shifted(rows, bits):
    zero = jnp.zeros_like(rows[0])
    count = len(rows)
    for position, chosen in enumerate(bits):
        step = 1 << position
        rows = [jnp.where(chosen, rows[t + step] if t + step < count else zero, rows[t]) for t in range(count)]
    return rows


def digits(offsets, most):
    return [(offsets >> position & 1) == 1 for position in range(most.bit_length())]


def merged(lower_rows, higher_rows, bits):
    return [x + y for x, y in zip(lower_rows, shifted(higher_rows, bits))]


def folded(rows, axis, half, bits):
    place = lax.broadcasted_iota(jnp.int32, rows[0].shape, axis)
    upper = (place & half) != 0
    facing = [jnp.take_along_axis(x, place ^ half, axis=axis) for x in rows]
    lower_rows = [jnp.where(upper, y, x) for x, y in zip(rows, facing)]
    higher_rows = [jnp.where(upper, x, y) for x, y in zip(rows, facing)]
    return merged(lower_rows, higher_rows, bits)


def tree_kernel(detected_ref, shifts_ref, out_ref, wide, held, turned):
    blocks, samples, width = out_ref.shape
    pieces = width // LANES
    scale = 1.0 / (8.0 * math.sqrt(NSUB))
    length = samples * pieces
    pitch = length + 8
    for q in range(blocks):
        wide[q * pitch : q * pitch + length] = detected_ref[q * length : (q + 1) * length].astype(jnp.float32)

    def bits_of(section, group, piece):
        offsets = shifts_ref[section, group * 8 : (group + 1) * 8, piece * LANES : (piece + 1) * LANES]
        return digits(offsets, min(1 << section, 8))

    lane_bits = LANES.bit_length() - 1
    for group in range(blocks // 8):
        for piece in range(pieces):
            rows = []
            for t in range(samples):
                first = group * 8 * pitch + t // 2 * 4 + piece * 2 + t % 2
                rows.append(wide[pl.ds(first, 8, stride=pitch), :])
            mean = functools.reduce(jnp.add, rows) * (1.0 / samples)
            rows = [row - mean for row in rows]
            for section in range(lane_bits):
                rows = folded(rows, 1, 1 << section, bits_of(section, group, piece))
            for t in range(samples):
                held[piece, group, t] = rows[t]
    for group in range(blocks // 8):
        for piece in range(pieces):
            lower_rows = [held[0, group, t] for t in range(samples)]
            higher_rows = [held[1, group, t] for t in range(samples)]
            rows = merged(lower_rows, higher_rows, bits_of(lane_bits, group, piece))
            for bit in range(3):
                section = lane_bits + 1 + bit
                rows = folded(rows, 0, 1 << bit, bits_of(section, group, piece))
            for t in range(samples):
                first = (group * pieces + piece) * samples * 8 + t * 8
                wide[first : first + 8, :] = rows[t]
    for piece in range(pieces):
        parts = []
        for group in range(2):
            first = (group * pieces + piece) * samples * 8
            parts.append([wide[first + t * 8 : first + t * 8 + 8, :] for t in range(samples)])
        for group in range(2):
            rows = merged(parts[0], parts[1], bits_of(lane_bits + 4, group, piece))
            for t in range(samples):
                turned[piece, pl.ds(group * 8 * PITCH + t, 8, stride=PITCH), :] = rows[t] * scale
        for q in range(blocks):
            block = turned[piece, q * PITCH : q * PITCH + samples, :]
            out_ref[q, :, piece * LANES : (piece + 1) * LANES] = block.astype(jnp.bfloat16)


def tree(detected, shifts):
    sections, blocks, width = shifts.shape
    pieces = width // LANES
    rows = detected.shape[0]
    return pl.pallas_call(
        tree_kernel,
        out_shape=jax.ShapeDtypeStruct((blocks, TIME, width), jnp.bfloat16),
        scratch_shapes=[
            pltpu.VMEM((rows + 8 * blocks, LANES), jnp.float32),
            pltpu.VMEM((pieces, blocks // 8, TIME, 8, LANES), jnp.float32),
            pltpu.VMEM((pieces, blocks * PITCH, LANES), jnp.float32),
        ],
        compiler_params=pltpu.CompilerParams(vmem_limit_bytes=8 * MIB),
        name="tree",
    )(detected, shifts)


def width_range(k):
    return (min(2 ** (k - 1) + 1, TIME), min(2**k, TIME)) if k else (1, 1)


def peaks_kernel(widths_ref, series_ref, same_hbm, peaks_hbm, wide, sums, best, same_sem, sems):
    beams, samples, width = series_ref.shape
    same = pltpu.make_async_copy(series_ref, same_hbm, same_sem)
    same.start()
    for j in range(width // LANES):
        lanes = slice(j * LANES, (j + 1) * LANES)
        wide[j] = series_ref[:, :, lanes].astype(jnp.float32).reshape(beams * samples, LANES)
        total = jnp.zeros((beams, LANES), jnp.float32)
        sums[0, :, lanes] = total
        for t in range(samples):
            total = total + wide[j, pl.ds(t, beams, stride=samples), :]
            sums[t + 1, :, lanes] = total
    for t in range(samples + 1, sums.shape[0]):
        sums[t] = jnp.full((beams, width), -1e30, jnp.float32)
    copies = []
    for k in range(best.shape[0]):
        reach = widths_ref[k]
        value = sums[reach]
        for t in range(1, samples + 1 - width_range(k)[0]):
            value = jnp.maximum(value, sums[t + reach] - sums[t])
        best[k] = value / jnp.sqrt(jnp.full((beams, width), reach).astype(jnp.float32))
        copies.append(pltpu.make_async_copy(best.at[k], peaks_hbm.at[k], sems.at[k]))
        copies[-1].start()
    same.wait()
    for copy in copies:
        copy.wait()


def peaks(widths, series):
    beams, samples, width = series.shape
    count = widths.shape[0]
    rows = max(samples + 1 - low + high for low, high in map(width_range, range(count)))
    return pl.pallas_call(
        peaks_kernel,
        in_specs=[pl.BlockSpec(memory_space=pltpu.SMEM), pl.BlockSpec(memory_space=pltpu.VMEM)],
        out_specs=[pl.BlockSpec(memory_space=pltpu.HBM)] * 2,
        out_shape=[
            jax.ShapeDtypeStruct(series.shape, series.dtype),
            jax.ShapeDtypeStruct((count, beams, width), jnp.float32),
        ],
        scratch_shapes=[
            pltpu.VMEM((width // LANES, beams * samples, LANES), jnp.float32),
            pltpu.VMEM((rows, beams, width), jnp.float32),
            pltpu.VMEM((count, beams, width), jnp.float32),
            pltpu.SemaphoreType.DMA,
            pltpu.SemaphoreType.DMA((count,)),
        ],
        compiler_params=pltpu.CompilerParams(vmem_limit_bytes=8 * MIB),
        name="peaks",
    )(widths, series)


def exchanged(block, axes):
    return lax.all_to_all(block, axes, split_axis=0, concat_axis=0, tiled=True)


def shards(voltages, gains, shifts, widths):
    groups = lax.axis_size("beam")
    place = lax.axis_index("beam").astype(jnp.int32)
    chip, core = place >> 1, place & 1
    swap = [(i, i ^ 1) for i in range(groups)]
    other = [lax.ppermute(block, "beam", swap) for block in (voltages, gains)]
    messages = calibrate(chip, core, *other, calibrate(chip, core, voltages, gains))

    def sent(block, distance):
        return lax.ppermute(block, "beam", [(i, (i + distance * CORES) % groups) for i in range(groups)])

    got = list(messages)
    for k in (1, 7, 2, 6, 4):
        got[k] = sent(messages[k], k)
    third, fifth, got[1], got[7] = lax.optimization_barrier((messages[3], messages[5], got[1], got[7]))
    got[3], got[5] = sent(third, 3), sent(fifth, 5)
    got[2], got[6], chip, shifts, widths = lax.optimization_barrier((got[2], got[6], chip, shifts, widths))
    short = jnp.concatenate([shifts.astype(jnp.bfloat16), jnp.zeros((16 - shifts.shape[0], shifts.shape[1]), jnp.bfloat16)])
    table = exchanged(jnp.broadcast_to(short[None], (lax.axis_size("freq"),) + short.shape), "freq")
    table = jnp.transpose(table[:, : shifts.shape[0]].astype(jnp.int32), (1, 0, 2))
    early = (steering(groups, chip), jnp.maximum(widths, 1), table)
    received, matrix, reach, table = lax.optimization_barrier((got, *early))
    detected = detect(received, matrix)
    spread = exchanged(detected.reshape(FEEDS, -1, LANES), ("freq", "beam"))
    series = exchanged(tree(spread.reshape(detected.shape), table), "freq")
    return tuple(peaks(reach, series))


def solution(mesh):
    return jax.shard_map(
        shards,
        mesh=mesh,
        in_specs=(P(None, "beam", None, "freq"), P(None, "beam", "freq"), P(None, "freq"), P()),
        out_specs=(P("beam", None, "freq"), P(None, "beam", "freq")),
        check_vma=False,
    )
```

```python
import functools
import math

import jax
import jax.numpy as jnp
from jax import lax
from jax.experimental import pallas as pl
from jax.experimental.pallas import tpu as pltpu
from jax.sharding import PartitionSpec as P

FEEDS = 256
CHAN_SUM = 4
NSUB = 4096
TIME = 16
LANES = 128
PITCH = 24
MIB = 1024 * 1024


def steering(groups):
    size = FEEDS // groups
    row = lax.broadcasted_iota(jnp.int32, (2 * FEEDS, 2 * FEEDS), 0)
    col = lax.broadcasted_iota(jnp.int32, (2 * FEEDS, 2 * FEEDS), 1)
    out_part = row // FEEDS
    beam = row % groups * size + row % FEEDS // groups
    feed = col // (2 * size) * size + col % size
    in_part = col // size % 2
    angles = (beam * feed % FEEDS).astype(jnp.float32) * (2.0 * math.pi / FEEDS)
    factor = 1.0 / math.sqrt(FEEDS)
    cosine = jnp.cos(angles) * factor
    sine = jnp.sin(angles) * factor
    value = jnp.where(in_part == out_part, cosine, jnp.where(out_part == 0, sine, -sine))
    return value.astype(jnp.bfloat16)


def calibrate_kernel(volt_hbm, gain_hbm, out_hbm, volt, gain, wide, done, in_sems, out_sems):
    chunks, _, feeds, samples, _ = volt.shape

    def arriving(j):
        lanes = pl.ds(j * LANES, LANES)
        return (
            pltpu.make_async_copy(volt_hbm.at[:, :, :, lanes], volt.at[j], in_sems.at[0, j]),
            pltpu.make_async_copy(gain_hbm.at[:, :, lanes], gain.at[j], in_sems.at[1, j]),
        )

    def leaving(j):
        return pltpu.make_async_copy(done.at[j], out_hbm.at[:, :, pl.ds(j * LANES, LANES)], out_sems.at[j])

    for j in range(chunks):
        for copy in arriving(j):
            copy.start()
    for j in range(chunks):
        for copy in arriving(j):
            copy.wait()
        for part in range(2):
            block = volt[j, part].astype(jnp.float32)
            for f in range(feeds):
                wide[j, part, f * PITCH : f * PITCH + samples] = block[f]
        gain_re = gain[j, 0]
        gain_im = gain[j, 1]
        for t in range(samples):
            volt_re = wide[j, 0, pl.ds(t, feeds, stride=PITCH), :]
            volt_im = wide[j, 1, pl.ds(t, feeds, stride=PITCH), :]
            real = gain_re * volt_re - gain_im * volt_im
            imag = gain_re * volt_im + gain_im * volt_re
            done[j, t, :feeds] = real.astype(jnp.bfloat16)
            done[j, t, feeds:] = imag.astype(jnp.bfloat16)
        leaving(j).start()
    for j in range(chunks):
        leaving(j).wait()


def calibrate(voltages, gains):
    _, feeds, samples, width = voltages.shape
    chunks = width // LANES
    return pl.pallas_call(
        calibrate_kernel,
        in_specs=[pl.BlockSpec(memory_space=pl.ANY)] * 2,
        out_specs=pl.BlockSpec(memory_space=pltpu.HBM),
        out_shape=jax.ShapeDtypeStruct((samples, 2 * feeds, width), jnp.bfloat16),
        scratch_shapes=[
            pltpu.VMEM((chunks, 2, feeds, samples, LANES), jnp.bfloat16),
            pltpu.VMEM((chunks, 2, feeds, LANES), jnp.float32),
            pltpu.VMEM((chunks, 2, feeds * PITCH, LANES), jnp.float32),
            pltpu.VMEM((chunks, samples, 2 * feeds, LANES), jnp.bfloat16),
            pltpu.SemaphoreType.DMA((2, chunks)),
            pltpu.SemaphoreType.DMA((chunks,)),
        ],
        compiler_params=pltpu.CompilerParams(vmem_limit_bytes=60 * MIB),
        name="calibrate",
    )(voltages, gains)


def detect_kernel(matrix_ref, x_ref, out_ref, scratch):
    width = x_ref.shape[1]
    step = 256
    pieces = width // CHAN_SUM // LANES
    deep = CHAN_SUM * LANES
    picking = lax.broadcasted_iota(jnp.int32, (deep, LANES), 0) == lax.broadcasted_iota(jnp.int32, (deep, LANES), 1) * CHAN_SUM
    picking = picking.astype(jnp.bfloat16)
    for h in range(pieces):
        sums = []
        for first in range(h * deep, (h + 1) * deep, step):
            formed = jnp.dot(matrix_ref[...], x_ref[:, first : first + step], preferred_element_type=jnp.float32)
            power = formed[:FEEDS] * formed[:FEEDS] + formed[FEEDS:] * formed[FEEDS:]
            for lane in range(0, step, LANES):
                part = power[:, lane : lane + LANES]
                part = part + pltpu.roll(part, LANES - 1, 1)
                sums.append((part + pltpu.roll(part, LANES - 2, 1)).astype(jnp.bfloat16))
        summed = jnp.concatenate(sums, axis=1)
        scratch[pl.ds(h, FEEDS, stride=pieces), :] = jnp.dot(summed, picking, preferred_element_type=jnp.float32)
    out_ref[...] = scratch[...].astype(jnp.bfloat16)


def detect(received, matrix):
    shape = (FEEDS * received.shape[1] // CHAN_SUM // LANES, LANES)
    return pl.pallas_call(
        detect_kernel,
        out_shape=jax.ShapeDtypeStruct(shape, jnp.bfloat16),
        scratch_shapes=[pltpu.VMEM(shape, jnp.float32)],
        compiler_params=pltpu.CompilerParams(vmem_limit_bytes=16 * MIB),
        name="detect",
    )(matrix, received)


def shifted(rows, bits):
    zero = jnp.zeros_like(rows[0])
    count = len(rows)
    for position, chosen in enumerate(bits):
        step = 1 << position
        rows = [jnp.where(chosen, rows[t + step] if t + step < count else zero, rows[t]) for t in range(count)]
    return rows


def digits(offsets, most):
    return [(offsets >> position & 1) == 1 for position in range(most.bit_length())]


def merged(lower_rows, higher_rows, bits):
    return [x + y for x, y in zip(lower_rows, shifted(higher_rows, bits))]


def folded(rows, axis, half, bits):
    place = lax.broadcasted_iota(jnp.int32, rows[0].shape, axis)
    upper = (place & half) != 0
    facing = [jnp.take_along_axis(x, place ^ half, axis=axis) for x in rows]
    lower_rows = [jnp.where(upper, y, x) for x, y in zip(rows, facing)]
    higher_rows = [jnp.where(upper, x, y) for x, y in zip(rows, facing)]
    return merged(lower_rows, higher_rows, bits)


def tree_kernel(detected_ref, shifts_ref, out_ref, wide, held, turned):
    blocks, samples, width = out_ref.shape
    pieces = width // LANES
    scale = 1.0 / (8.0 * math.sqrt(NSUB))
    length = samples * pieces
    pitch = length + 8
    for q in range(blocks):
        wide[q * pitch : q * pitch + length] = detected_ref[q * length : (q + 1) * length].astype(jnp.float32)

    def bits_of(section, group, piece):
        offsets = shifts_ref[section, group * 8 : (group + 1) * 8, piece * LANES : (piece + 1) * LANES]
        return digits(offsets, min(1 << section, 8))

    lane_bits = LANES.bit_length() - 1
    for group in range(blocks // 8):
        for piece in range(pieces):
            rows = []
            for t in range(samples):
                first = group * 8 * pitch + t * pieces + piece
                rows.append(wide[pl.ds(first, 8, stride=pitch), :])
            mean = functools.reduce(jnp.add, rows) * (1.0 / samples)
            rows = [row - mean for row in rows]
            for section in range(lane_bits):
                rows = folded(rows, 1, 1 << section, bits_of(section, group, piece))
            for t in range(samples):
                held[piece, group, t] = rows[t]
    for group in range(blocks // 8):
        for piece in range(pieces):
            lower_rows = [held[0, group, t] for t in range(samples)]
            higher_rows = [held[1, group, t] for t in range(samples)]
            rows = merged(lower_rows, higher_rows, bits_of(lane_bits, group, piece))
            for bit in range(3):
                section = lane_bits + 1 + bit
                rows = folded(rows, 0, 1 << bit, bits_of(section, group, piece))
            for t in range(samples):
                first = (group * pieces + piece) * samples * 8 + t * 8
                wide[first : first + 8, :] = rows[t]
    for piece in range(pieces):
        parts = []
        for group in range(2):
            first = (group * pieces + piece) * samples * 8
            parts.append([wide[first + t * 8 : first + t * 8 + 8, :] for t in range(samples)])
        for group in range(2):
            rows = merged(parts[0], parts[1], bits_of(lane_bits + 4, group, piece))
            for t in range(samples):
                turned[piece, pl.ds(group * 8 * PITCH + t, 8, stride=PITCH), :] = rows[t] * scale
        for q in range(blocks):
            block = turned[piece, q * PITCH : q * PITCH + samples, :]
            out_ref[q, :, piece * LANES : (piece + 1) * LANES] = block.astype(jnp.bfloat16)


def tree(detected, shifts):
    sections, blocks, width = shifts.shape
    pieces = width // LANES
    rows = detected.shape[0]
    return pl.pallas_call(
        tree_kernel,
        out_shape=jax.ShapeDtypeStruct((blocks, TIME, width), jnp.bfloat16),
        scratch_shapes=[
            pltpu.VMEM((rows + 8 * blocks, LANES), jnp.float32),
            pltpu.VMEM((pieces, blocks // 8, TIME, 8, LANES), jnp.float32),
            pltpu.VMEM((pieces, blocks * PITCH, LANES), jnp.float32),
        ],
        compiler_params=pltpu.CompilerParams(vmem_limit_bytes=8 * MIB),
        name="tree",
    )(detected, shifts)


def width_range(k):
    return (min(2 ** (k - 1) + 1, TIME), min(2**k, TIME)) if k else (1, 1)


def peaks_kernel(widths_ref, series_ref, same_hbm, peaks_hbm, wide, sums, best, same_sem, sems):
    beams, samples, width = series_ref.shape
    same = pltpu.make_async_copy(series_ref, same_hbm, same_sem)
    same.start()
    for j in range(width // LANES):
        lanes = slice(j * LANES, (j + 1) * LANES)
        block = series_ref[:, :, lanes].astype(jnp.float32)
        for b in range(beams):
            wide[j, b * PITCH : b * PITCH + samples] = block[b]
        total = jnp.zeros((beams, LANES), jnp.float32)
        sums[0, :, lanes] = total
        for t in range(samples):
            total = total + wide[j, pl.ds(t, beams, stride=PITCH), :]
            sums[t + 1, :, lanes] = total
    for t in range(samples + 1, sums.shape[0]):
        sums[t] = jnp.full((beams, width), -1e30, jnp.float32)
    copies = []
    for k in range(best.shape[0]):
        reach = widths_ref[k]
        value = sums[reach]
        for t in range(1, samples + 1 - width_range(k)[0]):
            value = jnp.maximum(value, sums[t + reach] - sums[t])
        best[k] = value / jnp.sqrt(jnp.full((beams, width), reach).astype(jnp.float32))
        copies.append(pltpu.make_async_copy(best.at[k], peaks_hbm.at[k], sems.at[k]))
        copies[-1].start()
    same.wait()
    for copy in copies:
        copy.wait()


def peaks(widths, series):
    beams, samples, width = series.shape
    count = widths.shape[0]
    rows = max(samples + 1 - low + high for low, high in map(width_range, range(count)))
    return pl.pallas_call(
        peaks_kernel,
        in_specs=[pl.BlockSpec(memory_space=pltpu.SMEM), pl.BlockSpec(memory_space=pltpu.VMEM)],
        out_specs=[pl.BlockSpec(memory_space=pltpu.HBM)] * 2,
        out_shape=[
            jax.ShapeDtypeStruct(series.shape, series.dtype),
            jax.ShapeDtypeStruct((count, beams, width), jnp.float32),
        ],
        scratch_shapes=[
            pltpu.VMEM((width // LANES, beams * PITCH, LANES), jnp.float32),
            pltpu.VMEM((rows, beams, width), jnp.float32),
            pltpu.VMEM((count, beams, width), jnp.float32),
            pltpu.SemaphoreType.DMA,
            pltpu.SemaphoreType.DMA((count,)),
        ],
        compiler_params=pltpu.CompilerParams(vmem_limit_bytes=8 * MIB),
        name="peaks",
    )(widths, series)


def gathered(block, axis):
    count = lax.axis_size(axis)
    position = lax.axis_index(axis)
    whole = block[None]
    step = 1
    while step < count:
        parts = [whole]
        for k in range(1, 4):
            parts.append(lax.ppermute(whole, axis, [(i, i ^ k * step) for i in range(count)]))
        for bit in (1, 2):
            odd = position & bit * step != 0
            parts = [jnp.where(odd, parts[k ^ bit], parts[k]) for k in range(4)]
        whole = jnp.concatenate(parts)
        step *= 4
    return whole


def exchanged(block, axes):
    return lax.all_to_all(block, axes, split_axis=0, concat_axis=0, tiled=True)


def shards(voltages, gains, shifts, widths):
    groups = lax.axis_size("beam")
    received = exchanged(calibrate(voltages, gains), "beam")
    matrix, shifts = lax.optimization_barrier((steering(groups), shifts))
    table = jnp.transpose(gathered(shifts, "freq"), (1, 0, 2))
    early = (matrix, table, jnp.maximum(widths, 1))
    received, matrix, table, reach = lax.optimization_barrier((received, *early))
    detected = detect(received.reshape(2 * FEEDS, received.shape[2]), matrix)
    spread = exchanged(detected.reshape(FEEDS, -1, LANES), ("freq", "beam"))
    series = exchanged(tree(spread.reshape(detected.shape), table), "freq")
    return tuple(peaks(reach, series))


def solution(mesh):
    return jax.shard_map(
        shards,
        mesh=mesh,
        in_specs=(P(None, "beam", None, "freq"), P(None, "beam", "freq"), P(None, "freq"), P()),
        out_specs=(P("beam", None, "freq"), P(None, "beam", "freq")),
        check_vma=False,
    )
```

```python
import functools
import math

import jax
import jax.numpy as jnp
from jax import lax
from jax.experimental import pallas as pl
from jax.experimental.pallas import tpu as pltpu
from jax.sharding import PartitionSpec as P

FEEDS = 256
CHAN_SUM = 4
NSUB = 4096
TIME = 16
LANES = 128
PITCH = 24
MIB = 1024 * 1024


def steering(groups):
    size = FEEDS // groups
    row = lax.broadcasted_iota(jnp.int32, (2 * FEEDS, 2 * FEEDS), 0)
    col = lax.broadcasted_iota(jnp.int32, (2 * FEEDS, 2 * FEEDS), 1)
    out_part = row // FEEDS
    beam = row % groups * size + row % FEEDS // groups
    feed = col // (2 * size) * size + col % size
    in_part = col // size % 2
    angles = (beam * feed % FEEDS).astype(jnp.float32) * (2.0 * math.pi / FEEDS)
    factor = 1.0 / math.sqrt(FEEDS)
    cosine = jnp.cos(angles) * factor
    sine = jnp.sin(angles) * factor
    value = jnp.where(in_part == out_part, cosine, jnp.where(out_part == 0, sine, -sine))
    return value.astype(jnp.bfloat16)


def calibrate_kernel(volt_hbm, gain_hbm, out_hbm, volt, gain, wide, done, in_sems, out_sems):
    chunks, _, feeds, samples, _ = volt.shape

    def arriving(j):
        lanes = pl.ds(j * LANES, LANES)
        return (
            pltpu.make_async_copy(volt_hbm.at[:, :, :, lanes], volt.at[j], in_sems.at[0, j]),
            pltpu.make_async_copy(gain_hbm.at[:, :, lanes], gain.at[j], in_sems.at[1, j]),
        )

    def leaving(j):
        return pltpu.make_async_copy(done.at[j], out_hbm.at[:, :, pl.ds(j * LANES, LANES)], out_sems.at[j])

    for j in range(chunks):
        for copy in arriving(j):
            copy.start()
    for j in range(chunks):
        for copy in arriving(j):
            copy.wait()
        for part in range(2):
            block = volt[j, part].astype(jnp.float32)
            for f in range(feeds):
                wide[j, part, f * PITCH : f * PITCH + samples] = block[f]
        gain_re = gain[j, 0]
        gain_im = gain[j, 1]
        for t in range(samples):
            volt_re = wide[j, 0, pl.ds(t, feeds, stride=PITCH), :]
            volt_im = wide[j, 1, pl.ds(t, feeds, stride=PITCH), :]
            real = gain_re * volt_re - gain_im * volt_im
            imag = gain_re * volt_im + gain_im * volt_re
            done[j, t, :feeds] = real.astype(jnp.bfloat16)
            done[j, t, feeds:] = imag.astype(jnp.bfloat16)
        leaving(j).start()
    for j in range(chunks):
        leaving(j).wait()


def calibrate(voltages, gains):
    _, feeds, samples, width = voltages.shape
    chunks = width // LANES
    return pl.pallas_call(
        calibrate_kernel,
        in_specs=[pl.BlockSpec(memory_space=pl.ANY)] * 2,
        out_specs=pl.BlockSpec(memory_space=pltpu.HBM),
        out_shape=jax.ShapeDtypeStruct((samples, 2 * feeds, width), jnp.bfloat16),
        scratch_shapes=[
            pltpu.VMEM((chunks, 2, feeds, samples, LANES), jnp.bfloat16),
            pltpu.VMEM((chunks, 2, feeds, LANES), jnp.float32),
            pltpu.VMEM((chunks, 2, feeds * PITCH, LANES), jnp.float32),
            pltpu.VMEM((chunks, samples, 2 * feeds, LANES), jnp.bfloat16),
            pltpu.SemaphoreType.DMA((2, chunks)),
            pltpu.SemaphoreType.DMA((chunks,)),
        ],
        compiler_params=pltpu.CompilerParams(vmem_limit_bytes=60 * MIB),
        name="calibrate",
    )(voltages, gains)


def detect_kernel(matrix_ref, x_ref, out_ref, scratch):
    width = x_ref.shape[1]
    step = 256
    pieces = width // CHAN_SUM // LANES
    deep = CHAN_SUM * LANES
    picking = lax.broadcasted_iota(jnp.int32, (deep, LANES), 0) == lax.broadcasted_iota(jnp.int32, (deep, LANES), 1) * CHAN_SUM
    picking = picking.astype(jnp.bfloat16)
    for h in range(pieces):
        sums = []
        for first in range(h * deep, (h + 1) * deep, step):
            formed = jnp.dot(matrix_ref[...], x_ref[:, first : first + step], preferred_element_type=jnp.float32)
            power = formed[:FEEDS] * formed[:FEEDS] + formed[FEEDS:] * formed[FEEDS:]
            for lane in range(0, step, LANES):
                part = power[:, lane : lane + LANES]
                part = part + pltpu.roll(part, LANES - 1, 1)
                sums.append((part + pltpu.roll(part, LANES - 2, 1)).astype(jnp.bfloat16))
        summed = jnp.concatenate(sums, axis=1)
        scratch[pl.ds(h, FEEDS, stride=pieces), :] = jnp.dot(summed, picking, preferred_element_type=jnp.float32)
    out_ref[...] = scratch[...].astype(jnp.bfloat16)


def detect(received, matrix):
    shape = (FEEDS * received.shape[1] // CHAN_SUM // LANES, LANES)
    return pl.pallas_call(
        detect_kernel,
        out_shape=jax.ShapeDtypeStruct(shape, jnp.bfloat16),
        scratch_shapes=[pltpu.VMEM(shape, jnp.float32)],
        compiler_params=pltpu.CompilerParams(vmem_limit_bytes=16 * MIB),
        name="detect",
    )(matrix, received)


def shifted(rows, bits):
    zero = jnp.zeros_like(rows[0])
    count = len(rows)
    for position, chosen in enumerate(bits):
        step = 1 << position
        rows = [jnp.where(chosen, rows[t + step] if t + step < count else zero, rows[t]) for t in range(count)]
    return rows


def digits(offsets, most):
    return [(offsets >> position & 1) == 1 for position in range(most.bit_length())]


def merged(lower_rows, higher_rows, bits):
    return [x + y for x, y in zip(lower_rows, shifted(higher_rows, bits))]


def folded(rows, axis, half, bits):
    place = lax.broadcasted_iota(jnp.int32, rows[0].shape, axis)
    if axis == 0:
        lower_rows = [jnp.take_along_axis(x, place & ~half, axis=axis) for x in rows]
        higher_rows = [jnp.take_along_axis(x, place | half, axis=axis) for x in rows]
    else:
        upper = (place & half) != 0
        facing = [jnp.take_along_axis(x, place ^ half, axis=axis) for x in rows]
        lower_rows = [jnp.where(upper, y, x) for x, y in zip(rows, facing)]
        higher_rows = [jnp.where(upper, x, y) for x, y in zip(rows, facing)]
    return merged(lower_rows, higher_rows, bits)


def tree_kernel(detected_ref, shifts_ref, out_ref, wide, held, turned):
    blocks, samples, width = out_ref.shape
    pieces = width // LANES
    scale = 1.0 / (8.0 * math.sqrt(NSUB))
    length = samples * pieces
    pitch = length + 8
    for q in range(blocks):
        wide[q * pitch : q * pitch + length] = detected_ref[q * length : (q + 1) * length].astype(jnp.float32)

    def bits_of(section, group, piece):
        offsets = shifts_ref[section, group * 8 : (group + 1) * 8, piece * LANES : (piece + 1) * LANES]
        return digits(offsets, min(1 << section, 8))

    lane_bits = LANES.bit_length() - 1
    for group in range(blocks // 8):
        for piece in range(pieces):
            rows = []
            for t in range(samples):
                first = group * 8 * pitch + t * pieces + piece
                rows.append(wide[pl.ds(first, 8, stride=pitch), :])
            mean = functools.reduce(jnp.add, rows) * (1.0 / samples)
            rows = [row - mean for row in rows]
            for section in range(lane_bits):
                rows = folded(rows, 1, 1 << section, bits_of(section, group, piece))
            for t in range(samples):
                held[piece, group, t] = rows[t]
    for group in range(blocks // 8):
        for piece in range(pieces):
            lower_rows = [held[0, group, t] for t in range(samples)]
            higher_rows = [held[1, group, t] for t in range(samples)]
            rows = merged(lower_rows, higher_rows, bits_of(lane_bits, group, piece))
            for bit in range(3):
                section = lane_bits + 1 + bit
                rows = folded(rows, 0, 1 << bit, bits_of(section, group, piece))
            for t in range(samples):
                first = (group * pieces + piece) * samples * 8 + t * 8
                wide[first : first + 8, :] = rows[t]
    for piece in range(pieces):
        parts = []
        for group in range(2):
            first = (group * pieces + piece) * samples * 8
            parts.append([wide[first + t * 8 : first + t * 8 + 8, :] for t in range(samples)])
        for group in range(2):
            rows = merged(parts[0], parts[1], bits_of(lane_bits + 4, group, piece))
            for t in range(samples):
                turned[piece, pl.ds(group * 8 * PITCH + t, 8, stride=PITCH), :] = rows[t] * scale
        for q in range(blocks):
            block = turned[piece, q * PITCH : q * PITCH + samples, :]
            out_ref[q, :, piece * LANES : (piece + 1) * LANES] = block.astype(jnp.bfloat16)


def tree(detected, shifts):
    sections, blocks, width = shifts.shape
    pieces = width // LANES
    rows = detected.shape[0]
    return pl.pallas_call(
        tree_kernel,
        out_shape=jax.ShapeDtypeStruct((blocks, TIME, width), jnp.bfloat16),
        scratch_shapes=[
            pltpu.VMEM((rows + 8 * blocks, LANES), jnp.float32),
            pltpu.VMEM((pieces, blocks // 8, TIME, 8, LANES), jnp.float32),
            pltpu.VMEM((pieces, blocks * PITCH, LANES), jnp.float32),
        ],
        compiler_params=pltpu.CompilerParams(vmem_limit_bytes=8 * MIB),
        name="tree",
    )(detected, shifts)


def width_range(k):
    return (min(2 ** (k - 1) + 1, TIME), min(2**k, TIME)) if k else (1, 1)


def peaks_kernel(widths_ref, series_ref, same_hbm, peaks_hbm, wide, sums, best, same_sem, sems):
    beams, samples, width = series_ref.shape
    same = pltpu.make_async_copy(series_ref, same_hbm, same_sem)
    same.start()
    for j in range(width // LANES):
        lanes = slice(j * LANES, (j + 1) * LANES)
        block = series_ref[:, :, lanes].astype(jnp.float32)
        for b in range(beams):
            wide[j, b * PITCH : b * PITCH + samples] = block[b]
        total = jnp.zeros((beams, LANES), jnp.float32)
        sums[0, :, lanes] = total
        for t in range(samples):
            total = total + wide[j, pl.ds(t, beams, stride=PITCH), :]
            sums[t + 1, :, lanes] = total
    for t in range(samples + 1, sums.shape[0]):
        sums[t] = jnp.full((beams, width), -1e30, jnp.float32)
    copies = []
    for k in range(best.shape[0]):
        reach = widths_ref[k]
        value = sums[reach]
        for t in range(1, samples + 1 - width_range(k)[0]):
            value = jnp.maximum(value, sums[t + reach] - sums[t])
        best[k] = value / jnp.sqrt(jnp.full((beams, width), reach).astype(jnp.float32))
        copies.append(pltpu.make_async_copy(best.at[k], peaks_hbm.at[k], sems.at[k]))
        copies[-1].start()
    same.wait()
    for copy in copies:
        copy.wait()


def peaks(widths, series):
    beams, samples, width = series.shape
    count = widths.shape[0]
    rows = max(samples + 1 - low + high for low, high in map(width_range, range(count)))
    return pl.pallas_call(
        peaks_kernel,
        in_specs=[pl.BlockSpec(memory_space=pltpu.SMEM), pl.BlockSpec(memory_space=pltpu.VMEM)],
        out_specs=[pl.BlockSpec(memory_space=pltpu.HBM)] * 2,
        out_shape=[
            jax.ShapeDtypeStruct(series.shape, series.dtype),
            jax.ShapeDtypeStruct((count, beams, width), jnp.float32),
        ],
        scratch_shapes=[
            pltpu.VMEM((width // LANES, beams * PITCH, LANES), jnp.float32),
            pltpu.VMEM((rows, beams, width), jnp.float32),
            pltpu.VMEM((count, beams, width), jnp.float32),
            pltpu.SemaphoreType.DMA,
            pltpu.SemaphoreType.DMA((count,)),
        ],
        compiler_params=pltpu.CompilerParams(vmem_limit_bytes=8 * MIB),
        name="peaks",
    )(widths, series)


def gathered(block, axis):
    count = lax.axis_size(axis)
    position = lax.axis_index(axis)
    whole = block[None]
    step = 1
    while step < count:
        parts = [whole]
        for k in range(1, 4):
            parts.append(lax.ppermute(whole, axis, [(i, i ^ k * step) for i in range(count)]))
        for bit in (1, 2):
            odd = position & bit * step != 0
            parts = [jnp.where(odd, parts[k ^ bit], parts[k]) for k in range(4)]
        whole = jnp.concatenate(parts)
        step *= 4
    return whole


def exchanged(block, axes):
    return lax.all_to_all(block, axes, split_axis=0, concat_axis=0, tiled=True)


def shards(voltages, gains, shifts, widths):
    groups = lax.axis_size("beam")
    received = exchanged(calibrate(voltages, gains), "beam")
    matrix, shifts = lax.optimization_barrier((steering(groups), shifts))
    table = jnp.transpose(gathered(shifts, "freq"), (1, 0, 2))
    early = (matrix, table, jnp.maximum(widths, 1))
    received, matrix, table, reach = lax.optimization_barrier((received, *early))
    detected = detect(received.reshape(2 * FEEDS, received.shape[2]), matrix)
    spread = exchanged(detected.reshape(FEEDS, -1, LANES), ("freq", "beam"))
    series = exchanged(tree(spread.reshape(detected.shape), table), "freq")
    return tuple(peaks(reach, series))


def solution(mesh):
    return jax.shard_map(
        shards,
        mesh=mesh,
        in_specs=(P(None, "beam", None, "freq"), P(None, "beam", "freq"), P(None, "freq"), P()),
        out_specs=(P("beam", None, "freq"), P(None, "beam", "freq")),
        check_vma=False,
    )
```
